32 devices in a mesh: region: 4 (over z), slab: 8 (over y, x, core).
Axes of the slice: x: 2, y: 2, z: 4, core: 2. Of those that a mesh axis runs over, the one named last changes fastest.
Arguments:
- records: bfloat16 [1024, 4096], P('region', 'slab'), may hold values from -6 to 6
- first_station: int32 [4096], P(('region', 'slab')), may hold values from 0 to 255
- second_region: int32 [4096, 1], P(('region', 'slab')), may hold values from 0 to 3; in each aligned block of 128 rows (0 to 127, 128 to 255, ...) at most 40 rows name the same one
- second_station: int32 [4096], P(('region', 'slab')), may hold values from 0 to 255
Outputs:
- stacks: bfloat16 [4096, 2048], P(('region', 'slab'))
The draws below stay inside these ranges and needn't reach their ends.
Inputs may be any that keep to these rules, and one draw needn't show every extreme that they name: `second_region`: no region is named by more than 40 pairs of one device.
All inputs are finite; a program needn't handle non-finite values.
Results may differ from the reference program's by a relative error of at most 0.0077.
Values may be sent and summed in bfloat16 or wider, within the bound.
No kernel may reach another device: no remote copies, remote signals or barrier semaphores. Data moves between devices by JAX's collectives and lax.ppermute only.
A program may use at most 64 MiB of HBM per device.

```python
import math
import jax
import jax.numpy as jnp
import numpy as np
from jax import lax

NFFT = 2048
BINS = 1024
SEG = 2
HALF = 4
PAIR_DEV = 128
CAP = 40
STA_REG = 256
STATIONS = 1024
PAIRS = 4096
N_REGION = 4
N_SLAB = 8


def plant(drawn, key, least, high):
    longest = drawn.shape.index(max(drawn.shape))
    spots = []
    for shift in (0, 1):
        where = [jax.random.randint(jax.random.fold_in(key, axis), (), 0, length) for axis, length in enumerate(drawn.shape)]
        where[longest] = (where[longest] + shift) % drawn.shape[longest]
        spots.append(tuple(where))
    return drawn.at[spots[0]].set(least).at[spots[1]].set(high)


def level_of(own_key, dims, pieces, smallest, top_value):
    loudness, own = 1.0, jax.random.fold_in(own_key, 6)
    for dim, parts in pieces:
        steps = jnp.exp(jax.random.uniform(jax.random.fold_in(own, dim), (parts,), jnp.float32, smallest / len(pieces), top_value / len(pieces)))
        loudness = loudness * jnp.repeat(steps, dims[dim] // parts).reshape([-1 if axis == dim else 1 for axis in range(len(dims))])
    return loudness


def routed_block(stream_key, own, number, rows, count, top, most, skew):
    order = jax.random.permutation(stream_key, count)
    heavy_load, common = load_shares(count, rows * top, most, skew, True), load_shares(count, rows * top, most, skew, False)
    places = jnp.arange(count)

    def named(tallies, rotation):
        used = int((tallies > 0).sum())
        fixed = max(1, used // 4)
        passed = fixed + (places - fixed + rotation * (used - fixed)) % max(1, count - fixed)
        return jnp.zeros((count,), jnp.int32).at[order[jnp.where(places < fixed, places, passed)]].set(jnp.asarray(tallies, jnp.int32))

    tallies = jnp.where(number % 4 == 0, named(heavy_load, number // 4), named(common, number - number // 4 - 1))
    mixed = jax.random.permutation(jax.random.fold_in(own, 3), count)
    donor, sink = mixed[0:count // 2 * 2:2], mixed[1:count // 2 * 2:2]
    slack = jnp.minimum(tallies[donor] - 1, most - tallies[sink]) // 2
    slack = jnp.where((donor == order[0]) | (sink == order[0]) | (tallies[sink] == 0), 0, jnp.maximum(slack, 0))
    passed = jax.random.randint(jax.random.fold_in(own, 4), (count // 2,), 0, 1 << 20) % (slack + 1)
    tallies = tallies.at[donor].add(-passed).at[sink].add(passed)
    labels = jnp.searchsorted(jnp.cumsum(tallies), jnp.arange(rows * top), side="right").astype(jnp.int32)
    grid = labels.reshape(top, rows).T
    grid = grid[jax.random.permutation(jax.random.fold_in(own, 1), rows)]
    rotation = jax.random.randint(jax.random.fold_in(own, 2), (rows, 1), 0, top)
    return jnp.take_along_axis(grid, (jnp.arange(top)[None, :] + rotation) % top, axis=1)


def load_shares(amount, total, bound, lean, full):
    portions = [(1 << 20) // math.isqrt(standing ** lean) + 1 for standing in range(1, amount + 1)]
    largest = bound if full else min(bound, max(-(-total // amount), total * portions[0] // sum(portions)))
    least = 1 if total - largest >= amount - 1 else 0
    holding, rest = [largest] + [least] * (amount - 1), total - largest - least * (amount - 1)
    while rest > 0:
        free = [i for i in range(1, amount) if holding[i] < largest] or [i for i in range(1, amount) if holding[i] < bound]
        whole, remaining = sum([portions[i] for i in free]), rest
        for i in free:
            extra = min(bound - holding[i], max(1, remaining * portions[i] // whole), rest)
            holding[i] = holding[i] + extra
            rest = rest - extra
    return np.array(holding)


def bell_draw(key, extent, width, limit, split=(), kind=jnp.bfloat16):
    result = jax.random.normal(key, extent, jnp.float32) * width
    if len(split) > 0:
        result = level_of(key, extent, split, -0.22, 0.18) * result
    return jnp.clip(result, min=-limit, max=limit).astype(kind)


def setup_inputs(seed: int = 0) -> dict:
    streams_of = jax.random.split(jax.random.key(seed), 5)
    records = bell_draw(streams_of[0], (STATIONS, SEG * NFFT), 1.0, 6.0, ((0, 4), (1, 8)))
    first_station = plant(jax.random.randint(streams_of[1], (PAIRS,), 0, STA_REG), jax.random.fold_in(streams_of[1], 1), 0, STA_REG - 1).astype(jnp.int32)
    second_region_keys = jax.random.split(jax.random.fold_in(streams_of[2], 1), PAIRS // PAIR_DEV)
    second_region_turns = jax.random.permutation(jax.random.fold_in(streams_of[2], 3), PAIRS // PAIR_DEV)
    second_region = jax.vmap(lambda own, number: routed_block(jax.random.fold_in(streams_of[2], 2), own, number, PAIR_DEV, N_REGION, 1, CAP, 2))(second_region_keys, second_region_turns).reshape((PAIRS, 1))
    second_station = plant(jax.random.randint(streams_of[3], (PAIRS,), 0, STA_REG), jax.random.fold_in(streams_of[3], 1), 0, STA_REG - 1).astype(jnp.int32)
    return dict(records=records, first_station=first_station, second_region=second_region, second_station=second_station)


def dft_table():
    sample = jnp.arange(NFFT, dtype=jnp.int32)[:, None]
    frequency = jnp.arange(BINS, dtype=jnp.int32)[None, :]
    phase = (sample * frequency % NFFT).astype(jnp.float32) * (2.0 * math.pi / NFFT)
    return jnp.concatenate([jnp.cos(phase), -jnp.sin(phase)], axis=1).astype(jnp.bfloat16)

def whitened(traces):
    count = traces.shape[0]
    signal = traces.astype(jnp.float32).reshape(count * SEG, NFFT)
    signal = signal - lax.optimization_barrier(jnp.mean(signal, axis=1, keepdims=True))
    position = jnp.arange(NFFT, dtype=jnp.int32).astype(jnp.float32)
    taper = 0.5 - 0.5 * jnp.cos(position * (2.0 * math.pi / NFFT))
    tapered = (signal * taper[None, :]).astype(jnp.bfloat16)
    spectrum = jnp.dot(tapered, dft_table(), preferred_element_type=jnp.float32)
    real_part = spectrum[:, :BINS]
    imag_part = spectrum[:, BINS:]
    amplitude = jnp.sqrt(real_part * real_part + imag_part * imag_part + 1e-06)
    padded = jnp.pad(amplitude, ((0, 0), (HALF, HALF)))
    smooth = jnp.zeros_like(amplitude)
    for offset in range(2 * HALF + 1):
        smooth = smooth + padded[:, offset:offset + BINS]
    smooth = smooth / (2 * HALF + 1)
    level = lax.optimization_barrier(jnp.mean(amplitude, axis=1, keepdims=True))
    divisor = smooth + level + 1e-06
    white = spectrum / jnp.concatenate([divisor, divisor], axis=1)
    return white.astype(jnp.bfloat16).reshape(count, SEG * NFFT)

def cross(first_rows, second_rows):
    left = first_rows.astype(jnp.float32).reshape(first_rows.shape[:-1] + (SEG, 2, BINS))
    right = second_rows.astype(jnp.float32).reshape(second_rows.shape[:-1] + (SEG, 2, BINS))
    real_sum = lax.optimization_barrier(jnp.mean(left[..., 0, :] * right[..., 0, :] + left[..., 1, :] * right[..., 1, :], axis=-2))
    imag_sum = lax.optimization_barrier(jnp.mean(left[..., 0, :] * right[..., 1, :] - left[..., 1, :] * right[..., 0, :], axis=-2))
    return jnp.concatenate([real_sum, imag_sum], axis=-1).astype(jnp.bfloat16)

def reference(records, first_station, second_region, second_station):
    white = whitened(records)
    blocks = N_REGION * N_SLAB
    owner = jnp.arange(blocks, dtype=jnp.int32) // N_SLAB
    firsts = first_station.reshape(blocks, PAIR_DEV)
    seconds = (second_region[:, 0] * STA_REG + second_station).reshape(blocks, PAIR_DEV)

    def one_block(item):
        owner_region, first_ids, second_ids = item
        first_rows = jnp.take(white, owner_region * STA_REG + first_ids, axis=0)
        second_rows = jnp.take(white, second_ids, axis=0)
        return cross(first_rows, second_rows)
    stacked = lax.map(one_block, (owner, firsts, seconds))
    return stacked.reshape(PAIRS, NFFT)
```

```python
import functools
import math

import jax
import jax.numpy as jnp
import numpy as np
from jax import lax
from jax.experimental import pallas as pl
from jax.experimental.pallas import tpu as pltpu
from jax.sharding import PartitionSpec as P

NFFT = 2048
BINS = 1024
SEG = 2
HALF = 4
LANES = 128
INDEX_ROWS = 8
EXACT = 256
AXES = ("region", "slab")


def folded_tables():
    half = NFFT // 2
    sample = np.arange(half, dtype=np.int64)[:, None]
    tables = []
    for parity in (0, 1):
        frequency = 2 * np.arange(half // 2, dtype=np.int64)[None, :] + parity
        phase = (sample * frequency % NFFT) * (2.0 * math.pi / NFFT)
        tables.append(np.concatenate([np.cos(phase), -np.sin(phase)], axis=1).astype(jnp.bfloat16))
    return tables


def interleaver():
    order = np.zeros((2 * LANES, 2 * LANES), np.float32)
    place = np.arange(LANES)
    order[place, 2 * place] = 1.0
    order[LANES + place, 2 * place + 1] = 1.0
    return order.astype(jnp.bfloat16)


def taper_row():
    position = np.arange(NFFT, dtype=np.float64)
    return (0.5 - 0.5 * np.cos(position * (2.0 * math.pi / NFFT))).astype(np.float32)[None, :]


def shifted(values, step):
    width = values.shape[1]
    lane = lax.broadcasted_iota(jnp.int32, values.shape, 1)
    moved = pltpu.roll(values, (-step) % width, 1)
    return jnp.where((lane + step >= 0) & (lane + step < width), moved, 0.0)


def spectra_kernel(x_ref, index_ref, taper_ref, even_ref, odd_ref, order_ref, out_ref):
    slabs, count, _ = x_ref.shape
    per_segment = slabs // SEG
    half = NFFT // 2
    sums, differences = [], []
    for segment in range(SEG):
        pieces = [x_ref[segment * per_segment + j].astype(jnp.float32) for j in range(per_segment)]
        signal = jnp.concatenate(pieces, axis=1)
        signal = signal - jnp.sum(signal, axis=1, keepdims=True) * (1.0 / NFFT)
        signal = signal * taper_ref[...]
        sums.append((signal[:, :half] + signal[:, half:]).astype(jnp.bfloat16))
        differences.append((signal[:, :half] - signal[:, half:]).astype(jnp.bfloat16))
    quarter = half // 2
    even = jnp.dot(jnp.concatenate(sums, axis=0), even_ref[...], preferred_element_type=jnp.float32)
    odd = jnp.dot(jnp.concatenate(differences, axis=0), odd_ref[...], preferred_element_type=jnp.float32)
    size = []
    for part in (even, odd):
        real_part, imag_part = part[:, :quarter], part[:, quarter:]
        size.append(jnp.sqrt(real_part * real_part + imag_part * imag_part + 1e-06))
    level = (jnp.sum(size[0], axis=1, keepdims=True) + jnp.sum(size[1], axis=1, keepdims=True)) * (1.0 / BINS)
    e = {step: shifted(size[0], step) if step else size[0] for step in (-2, -1, 0, 1, 2)}
    o = {step: shifted(size[1], step) if step else size[1] for step in (-2, -1, 0, 1, 2)}
    even_inner, odd_inner = e[-1] + e[0] + e[1], o[-1] + o[0] + o[1]
    smooth_even = even_inner + e[-2] + e[2] + odd_inner + o[-2]
    smooth_odd = odd_inner + o[-2] + o[2] + even_inner + e[2]
    white = []
    for part, smooth in ((even, smooth_even), (odd, smooth_odd)):
        scale = 1.0 / (smooth * (1.0 / (2 * HALF + 1)) + level + 1e-06)
        white.append([(part[:, :quarter] * scale).astype(jnp.bfloat16), (part[:, quarter:] * scale).astype(jnp.bfloat16)])
    group = LANES // (2 * SEG)
    lane_group = lax.broadcasted_iota(jnp.int32, (count, LANES), 1) // group
    for j in range(BINS // (2 * LANES)):
        lanes = slice(j * LANES, (j + 1) * LANES)
        natural = []
        for kind in (0, 1):
            both = jnp.concatenate([white[0][kind][:, lanes], white[1][kind][:, lanes]], axis=1)
            natural.append(jnp.dot(both, order_ref[...], preferred_element_type=jnp.float32))
        for side in (0, 1):
            sources = [
                natural[kind][segment * count : (segment + 1) * count, side * LANES : (side + 1) * LANES]
                for segment in range(SEG)
                for kind in (0, 1)
            ]
            for q in range(2 * SEG):
                block = None
                for place, source in enumerate(sources):
                    turn = (place - q) * group % LANES
                    moved = pltpu.roll(source, turn, 1) if turn else source
                    block = moved if block is None else jnp.where(lane_group == place, moved, block)
                out_ref[(2 * j + side) * 2 * SEG + q, :count, :] = block.astype(jnp.bfloat16)
    for dest in range(out_ref.shape[0]):
        out_ref[dest, count:, :] = index_ref[...]


def cross_kernel(regions, slabs, table_ref, out_ref, flipped_ref):
    devices, rows, _ = table_ref.shape
    count = rows - INDEX_ROWS
    stations = slabs * count
    bins = LANES // (2 * SEG)
    per_step = 2
    for region in range(regions):
        block = table_ref[region * slabs : (region + 1) * slabs, :count, :].reshape(stations, LANES)
        flipped_ref[region * LANES : (region + 1) * LANES, :] = block.T
    station = lax.broadcasted_iota(jnp.int32, (stations, per_step * LANES), 0)

    def step(i, _):
        first_device = i * per_step

        def named(row):
            both = [table_ref[first_device + k, count : count + INDEX_ROWS, :].astype(jnp.float32)[row : row + 1] for k in range(per_step)]
            return jnp.concatenate(both, axis=1).astype(jnp.int32)

        first, second, target = named(0), named(1), named(2)
        pick_first = (station == first).astype(jnp.float32).astype(jnp.bfloat16)
        pick_second = (station == second).astype(jnp.float32).astype(jnp.bfloat16)
        home = first_device // slabs
        own = flipped_ref[pl.ds(pl.multiple_of(home * LANES, LANES), LANES), :]
        a = jnp.dot(own, pick_first, preferred_element_type=jnp.float32)
        b = None
        for region in range(regions):
            candidate = jnp.dot(flipped_ref[region * LANES : (region + 1) * LANES, :], pick_second, preferred_element_type=jnp.float32)
            b = candidate if b is None else jnp.where(target == region, candidate, b)
        real_sum, imag_sum = 0.0, 0.0
        for segment in range(SEG):
            at = 2 * segment * bins
            ar, ai = a[at : at + bins], a[at + bins : at + 2 * bins]
            br, bi = b[at : at + bins], b[at + bins : at + 2 * bins]
            real_sum = real_sum + (ar * br + ai * bi)
            imag_sum = imag_sum + (ar * bi - ai * br)
        real_sum = (real_sum * (1.0 / SEG)).astype(jnp.bfloat16)
        imag_sum = (imag_sum * (1.0 / SEG)).astype(jnp.bfloat16)
        for k in range(per_step):
            out_ref[first_device + k, :bins, :] = real_sum[:, k * LANES : (k + 1) * LANES]
            out_ref[first_device + k, bins:, :] = imag_sum[:, k * LANES : (k + 1) * LANES]
        return 0

    lax.fori_loop(0, devices // per_step, step, 0, unroll=2)


def place_kernel(in_ref, out_ref):
    devices, rows, _ = in_ref.shape
    bins = rows // 2
    sources = LANES // bins
    for kind in (0, 1):
        for j in range(devices // sources):
            block = in_ref[j * sources : (j + 1) * sources, kind * bins : (kind + 1) * bins, :]
            at = kind * BINS + j * LANES
            out_ref[:, at : at + LANES] = block.reshape(LANES, LANES).T


def by_bins(records, first_station, second_region, second_station):
    regions, slabs = lax.axis_size("region"), lax.axis_size("slab")
    devices = regions * slabs
    stations, samples = records.shape
    count = stations // slabs
    pair_count = first_station.shape[0]
    named = jnp.stack([first_station, second_station, second_region.reshape(-1)])
    index = jnp.pad(named, ((0, INDEX_ROWS - 3), (0, 0))).astype(jnp.bfloat16)
    arrived = lax.all_to_all(records.reshape(slabs, count, samples), "slab", split_axis=0, concat_axis=0, tiled=True)
    even, odd = folded_tables()
    vmem = pl.BlockSpec(memory_space=pltpu.VMEM)
    limit = pltpu.CompilerParams(vmem_limit_bytes=32 << 20)
    sent = pl.pallas_call(
        spectra_kernel,
        out_shape=jax.ShapeDtypeStruct((devices, count + INDEX_ROWS, LANES), jnp.bfloat16),
        in_specs=[vmem] * 6,
        out_specs=vmem,
        compiler_params=limit,
        name="spectra",
    )(arrived, index, jnp.asarray(taper_row()), jnp.asarray(even), jnp.asarray(odd), jnp.asarray(interleaver()))
    table = lax.all_to_all(sent, AXES, split_axis=0, concat_axis=0, tiled=True)
    partial = pl.pallas_call(
        functools.partial(cross_kernel, regions, slabs),
        out_shape=jax.ShapeDtypeStruct((devices, LANES // 2, pair_count), jnp.bfloat16),
        in_specs=[vmem],
        out_specs=vmem,
        scratch_shapes=[pltpu.VMEM((regions * LANES, stations), jnp.bfloat16)],
        compiler_params=limit,
        name="cross",
    )(table)
    pieces = lax.all_to_all(partial, AXES, split_axis=0, concat_axis=0, tiled=True)
    return pl.pallas_call(
        place_kernel,
        out_shape=jax.ShapeDtypeStruct((pair_count, 2 * BINS), jnp.bfloat16),
        in_specs=[vmem],
        out_specs=vmem,
        compiler_params=limit,
        name="place",
    )(pieces)


def dft_table():
    sample = jnp.arange(NFFT, dtype=jnp.int32)[:, None]
    frequency = jnp.arange(BINS, dtype=jnp.int32)[None, :]
    phase = (sample * frequency % NFFT).astype(jnp.float32) * (2.0 * math.pi / NFFT)
    return jnp.concatenate([jnp.cos(phase), -jnp.sin(phase)], axis=1).astype(jnp.bfloat16)


def whitened(traces):
    count = traces.shape[0]
    signal = traces.astype(jnp.float32).reshape(count * SEG, NFFT)
    signal = signal - jnp.mean(signal, axis=1, keepdims=True)
    position = jnp.arange(NFFT, dtype=jnp.int32).astype(jnp.float32)
    taper = 0.5 - 0.5 * jnp.cos(position * (2.0 * math.pi / NFFT))
    tapered = (signal * taper[None, :]).astype(jnp.bfloat16)
    spectrum = jnp.dot(tapered, dft_table(), preferred_element_type=jnp.float32)
    real_part = spectrum[:, :BINS]
    imag_part = spectrum[:, BINS:]
    amplitude = jnp.sqrt(real_part * real_part + imag_part * imag_part + 1e-06)
    padded = jnp.pad(amplitude, ((0, 0), (HALF, HALF)))
    smooth = jnp.zeros_like(amplitude)
    for offset in range(2 * HALF + 1):
        smooth = smooth + padded[:, offset : offset + BINS]
    smooth = smooth / (2 * HALF + 1)
    level = jnp.mean(amplitude, axis=1, keepdims=True)
    divisor = smooth + level + 1e-06
    white = spectrum / jnp.concatenate([divisor, divisor], axis=1)
    return white.astype(jnp.bfloat16).reshape(count, SEG * NFFT)


def cross(first_rows, second_rows):
    left = first_rows.astype(jnp.float32).reshape(first_rows.shape[:-1] + (SEG, 2, BINS))
    right = second_rows.astype(jnp.float32).reshape(second_rows.shape[:-1] + (SEG, 2, BINS))
    real_sum = jnp.mean(left[..., 0, :] * right[..., 0, :] + left[..., 1, :] * right[..., 1, :], axis=-2)
    imag_sum = jnp.mean(left[..., 0, :] * right[..., 1, :] - left[..., 1, :] * right[..., 0, :], axis=-2)
    return jnp.concatenate([real_sum, imag_sum], axis=-1).astype(jnp.bfloat16)


def by_rows(records, first_station, second_region, second_station):
    regions = lax.axis_size("region")
    pair_count = first_station.shape[0]
    capacity = max(2, pair_count // regions + pair_count // 16)
    arrived = lax.all_to_all(records, "slab", split_axis=0, concat_axis=1, tiled=True)
    spectra = whitened(arrived)
    width = spectra.shape[1]
    target = second_region[:, 0]
    onehot = (target[:, None] == jnp.arange(regions, dtype=jnp.int32)[None, :]).astype(jnp.int32)
    ranking = jnp.sum((jnp.cumsum(onehot, axis=0) - onehot) * onehot, axis=1)
    slot_index = target * capacity + ranking
    requests = jnp.zeros((regions * capacity,), jnp.int32).at[slot_index].set(second_station).reshape(regions, capacity)
    incoming = lax.all_to_all(requests, "region", split_axis=0, concat_axis=0, tiled=True)
    wanted = jnp.concatenate([first_station, incoming.reshape(-1)])
    piece = lax.all_gather(spectra, "slab", axis=0, tiled=True)
    picked = jnp.take(piece, wanted, axis=0)
    first_rows = picked[:pair_count]
    served = picked[pair_count:]
    returned = lax.all_to_all(
        served.reshape(regions, capacity, width), "region", split_axis=0, concat_axis=0, tiled=True
    )
    second_rows = jnp.take(returned.reshape(regions * capacity, width), slot_index, axis=0)
    return cross(first_rows, second_rows)


def local(records, first_station, second_region, second_station):
    devices = lax.axis_size("region") * lax.axis_size("slab")
    fits = 2 * SEG * BINS == LANES * devices and records.shape[0] <= EXACT and first_station.shape[0] == LANES
    plan = by_bins if fits else by_rows
    return plan(records, first_station, second_region, second_station)


def solution(mesh):
    placed = (
        P(AXES[0], AXES[1]),
        P(AXES),
        P(AXES, None),
        P(AXES),
    )
    return jax.shard_map(local, mesh=mesh, in_specs=placed, out_specs=P(AXES, None), check_vma=False)
```

```python
import functools
import math

import jax
import jax.numpy as jnp
import numpy as np
from jax import lax
from jax.experimental import pallas as pl
from jax.experimental.pallas import tpu as pltpu
from jax.sharding import PartitionSpec as P

NFFT = 2048
BINS = 1024
SEG = 2
HALF = 4
LANES = 128
INDEX_ROWS = 8
RADIX = 16
SMALL_ROWS = 40
EXACT = 256
AXES = ("region", "slab")


def constant_rows():
    fine = np.arange(LANES, dtype=np.int64)
    twiddle = np.arange(RADIX // 2 + 1)[:, None] * fine[None, :] * (2.0 * math.pi / NFFT)
    position = np.arange(NFFT, dtype=np.float64).reshape(RADIX, LANES)
    taper = 0.5 - 0.5 * np.cos(position * (2.0 * math.pi / NFFT))
    mirrored = fine >= LANES // 2
    frequency = np.where(mirrored, LANES - 1 - (fine - LANES // 2), fine)
    phase = (fine[:, None] * frequency[None, :] % LANES) * (2.0 * math.pi / LANES)
    sign = np.where(mirrored, -1.0, 1.0)
    real_side = np.concatenate([np.cos(phase), np.sin(phase)], axis=0)
    imag_side = np.concatenate([-np.sin(phase) * sign, np.cos(phase) * sign], axis=0)
    matrix = np.concatenate([real_side, imag_side], axis=0).astype(jnp.bfloat16)
    small = np.concatenate([np.cos(twiddle), np.sin(twiddle), taper], axis=0)
    small = np.pad(small, ((0, SMALL_ROWS - small.shape[0]), (0, 0)))
    return np.concatenate([small, matrix.astype(np.float64)], axis=0).astype(np.float32)


def prepare_kernel(index_in_ref, rows_ref, index_ref, small_ref, matrix_ref):
    index_ref[...] = index_in_ref[...]
    small_ref[...] = rows_ref[:SMALL_ROWS, :]
    for side in (0, 1):
        at = SMALL_ROWS + side * 2 * LANES
        matrix_ref[:, side * LANES : (side + 1) * LANES] = rows_ref[at : at + 2 * LANES, :].astype(jnp.bfloat16)


def short_dft(pieces):
    half = RADIX // 2
    a = [pieces[j] + pieces[j + half] for j in range(half)]
    b = [pieces[j] - pieces[j + half] for j in range(half)]
    f = [a[j] + a[j + 4] for j in range(4)]
    g = [a[j] - a[j + 4] for j in range(4)]
    out = [None] * (half + 1)
    even, odd = f[0] + f[2], f[1] + f[3]
    root = math.sqrt(0.5)
    minus, plus = root * (g[1] - g[3]), root * (g[1] + g[3])
    out[0], out[8] = (even + odd, None), (even - odd, None)
    out[4] = (f[0] - f[2], f[3] - f[1])
    out[2] = (g[0] + minus, -(g[2] + plus))
    out[6] = (g[0] - minus, g[2] - plus)
    d = {j: b[j] - b[half - j] for j in (1, 2, 3)}
    e = {j: b[j] + b[half - j] for j in (1, 2, 3)}
    for k in (1, 3, 5, 7):
        real_part, imag_part = b[0], (-b[4] if k % 4 == 1 else b[4])
        for j in (1, 2, 3):
            real_part = real_part + d[j] * math.cos(math.pi * j * k / half)
            imag_part = imag_part - e[j] * math.sin(math.pi * j * k / half)
        out[k] = (real_part, imag_part)
    return out


def smoothed(size, lane):
    left = lane < LANES // 2
    inside = (lane > 0) & (lane < LANES - 1)

    def turned(values, by):
        return pltpu.roll(values, by, 1)

    line = {t: size[t] for t in range(1, 8)}
    line[0] = jnp.where(left, size[0], jnp.where(inside, turned(size[0], LANES // 2 - 1), 0.0))
    line[8] = jnp.where(left, turned(size[0], LANES // 2), size[0])
    for i in range(1, HALF + 1):
        line[8 + i] = turned(size[8 - i], LANES // 2)
        wrapped = jnp.where(left, turned(size[i], LANES // 2 + 1), turned(size[i], LANES // 2 - 1))
        line[-i] = jnp.where(inside, wrapped, 0.0)
    two = {t: line[t] + line[t + 1] for t in range(-HALF, 8 + HALF)}
    four = {t: two[t] + two[t + 2] for t in range(-HALF, 8 + HALF - 2)}
    nine = [four[t - 4] + four[t] + line[t + 4] for t in range(0, 9)]
    return [jnp.where(left, nine[0], nine[8])] + nine[1:8]


def spectra_kernel(x_ref, index_ref, small_ref, matrix_ref, out_ref):
    slabs, count, samples = x_ref.shape
    per_segment, per_piece = slabs // SEG, samples // LANES
    rows = SEG * count
    pieces = []
    for j in range(per_segment):
        both = jnp.concatenate([x_ref[segment * per_segment + j] for segment in range(SEG)], axis=0).astype(jnp.float32)
        pieces += [both[:, i * LANES : (i + 1) * LANES] for i in range(per_piece)]
    total = pieces[0]
    for piece in pieces[1:]:
        total = total + piece
    mean = jnp.sum(total, axis=1, keepdims=True) * (1.0 / NFFT)
    taper = 2 * (RADIX // 2 + 1)
    pieces = [(piece - mean) * small_ref[taper + n1 : taper + n1 + 1, :] for n1, piece in enumerate(pieces)]
    turned = []
    for k1, (real_part, imag_part) in enumerate(short_dft(pieces)):
        cosine = small_ref[k1 : k1 + 1, :]
        sine = small_ref[RADIX // 2 + 1 + k1 : RADIX // 2 + 2 + k1, :]
        if imag_part is None:
            both = [real_part * cosine, -real_part * sine]
        else:
            both = [real_part * cosine + imag_part * sine, imag_part * cosine - real_part * sine]
        turned.append(jnp.concatenate([part.astype(jnp.bfloat16) for part in both], axis=1))
    spectrum = jnp.dot(jnp.concatenate(turned, axis=0), matrix_ref[...], preferred_element_type=jnp.float32)
    lane = lax.broadcasted_iota(jnp.int32, (rows, LANES), 1)
    real_parts, imag_parts = (
        [spectrum[k1 * rows : (k1 + 1) * rows, side * LANES : (side + 1) * LANES] for k1 in range(RADIX // 2 + 1)]
        for side in (0, 1)
    )
    real_parts = [jnp.where(lane < LANES // 2, real_parts[0], real_parts[8])] + real_parts[1:8]
    imag_parts = [jnp.where(lane < LANES // 2, imag_parts[0], imag_parts[8])] + imag_parts[1:8]
    size = [jnp.sqrt(re * re + im * im + 1e-06) for re, im in zip(real_parts, imag_parts)]
    total = size[0]
    for part in size[1:]:
        total = total + part
    level = jnp.sum(total, axis=1, keepdims=True) * (1.0 / BINS) + 1e-06
    group = LANES // (2 * SEG)
    lane_group = lane[:count] // group
    for s, smooth in enumerate(smoothed(size, lane)):
        scale = 1.0 / (smooth * (1.0 / (2 * HALF + 1)) + level)
        white = [real_parts[s] * scale, imag_parts[s] * scale]
        sources = [part[segment * count : (segment + 1) * count] for segment in range(SEG) for part in white]
        for q in range(2 * SEG):
            block = None
            for place, source in enumerate(sources):
                turn = (place - q) * group % LANES
                moved = pltpu.roll(source, turn, 1) if turn else source
                block = moved if block is None else jnp.where(lane_group == place, moved, block)
            out_ref[2 * SEG * s + q, :count, :] = block.astype(jnp.bfloat16)
    for dest in range(out_ref.shape[0]):
        out_ref[dest, count:, :] = index_ref[...]


def cross_kernel(regions, slabs, table_ref, out_ref, flipped_ref):
    devices, rows, _ = table_ref.shape
    count = rows - INDEX_ROWS
    stations = slabs * count
    bins = LANES // (2 * SEG)
    per_step = 2
    for region in range(regions):
        block = table_ref[region * slabs : (region + 1) * slabs, :count, :].reshape(stations, LANES)
        flipped_ref[region * LANES : (region + 1) * LANES, :] = block.T
    station = lax.broadcasted_iota(jnp.int32, (stations, per_step * LANES), 0).astype(jnp.float32).astype(jnp.bfloat16)
    one, zero = jnp.ones((), jnp.bfloat16), jnp.zeros((), jnp.bfloat16)
    for first_device in range(0, devices, per_step):
        named = [table_ref[first_device + k, count:, :] for k in range(per_step)]
        named = jnp.concatenate(named, axis=1)
        first, second, target = named[0:1], named[1:2], named[2:3].astype(jnp.float32)
        home = first_device // slabs
        own = flipped_ref[home * LANES : (home + 1) * LANES, :]
        a = jnp.dot(own, jnp.where(station == first, one, zero), preferred_element_type=jnp.float32)
        pick_second = jnp.where(station == second, one, zero)
        b = None
        for region in range(regions):
            rows_of = flipped_ref[region * LANES : (region + 1) * LANES, :]
            candidate = jnp.dot(rows_of, pick_second, preferred_element_type=jnp.float32)
            b = candidate if b is None else jnp.where(target == region, candidate, b)
        real_sum, imag_sum = 0.0, 0.0
        for segment in range(SEG):
            at = 2 * segment * bins
            ar, ai = a[at : at + bins], a[at + bins : at + 2 * bins]
            br, bi = b[at : at + bins], b[at + bins : at + 2 * bins]
            real_sum = real_sum + (ar * br + ai * bi)
            imag_sum = imag_sum + (ar * bi - ai * br)
        real_sum = (real_sum * (1.0 / SEG)).astype(jnp.bfloat16)
        imag_sum = (imag_sum * (1.0 / SEG)).astype(jnp.bfloat16)
        for k in range(per_step):
            out_ref[first_device + k, :bins, :] = real_sum[:, k * LANES : (k + 1) * LANES]
            out_ref[first_device + k, bins:, :] = imag_sum[:, k * LANES : (k + 1) * LANES]


def place_kernel(in_ref, out_ref):
    devices, rows, _ = in_ref.shape
    bins = rows // 2
    fine = LANES // RADIX
    row = lax.broadcasted_iota(jnp.int32, (LANES, LANES), 0)
    lane = lax.broadcasted_iota(jnp.int32, (LANES, LANES), 1)
    slab, side = row // (2 * fine), row // fine % 2
    k1 = jnp.where(side == 0, slab, jnp.where(slab == 0, RADIX // 2, RADIX - slab))
    order = (lane == k1 + RADIX * (row % fine)).astype(jnp.float32).astype(jnp.bfloat16)
    per_slab = devices // (RADIX // 2)
    per_side = per_slab // 2
    for kind in (0, 1):
        for j in range(BINS // LANES):
            group, at = divmod(j * fine, bins)
            at += kind * bins
            picked = [in_ref[u * per_side + group, at : at + fine, :] for u in range(RADIX)]
            block = jnp.concatenate(picked, axis=0).T
            natural = jnp.dot(block, order, preferred_element_type=jnp.float32)
            place = kind * BINS + j * LANES
            out_ref[:, place : place + LANES] = natural.astype(jnp.bfloat16)


def by_bins(records, first_station, second_region, second_station):
    regions, slabs = lax.axis_size("region"), lax.axis_size("slab")
    devices = regions * slabs
    stations, samples = records.shape
    count = stations // slabs
    pair_count = first_station.shape[0]
    arrived = lax.all_to_all(records.reshape(slabs, count, samples), "slab", split_axis=0, concat_axis=0, tiled=True)
    named = jnp.stack([first_station, second_station, second_region.reshape(-1)])
    index = jnp.pad(named, ((0, INDEX_ROWS - 3), (0, 0))).astype(jnp.bfloat16)
    vmem = pl.BlockSpec(memory_space=pltpu.VMEM)
    limit = pltpu.CompilerParams(vmem_limit_bytes=12 << 20)
    prepared = pl.pallas_call(
        prepare_kernel,
        out_shape=[
            jax.ShapeDtypeStruct(index.shape, jnp.bfloat16),
            jax.ShapeDtypeStruct((SMALL_ROWS, LANES), jnp.float32),
            jax.ShapeDtypeStruct((2 * LANES, 2 * LANES), jnp.bfloat16),
        ],
        in_specs=[vmem] * 2,
        out_specs=[vmem] * 3,
        compiler_params=limit,
        cost_estimate=pl.CostEstimate(flops=NFFT * BINS, bytes_accessed=NFFT * BINS, transcendentals=0),
        name="prepare",
    )(index, jnp.asarray(constant_rows()))
    sent = pl.pallas_call(
        spectra_kernel,
        out_shape=jax.ShapeDtypeStruct((devices, count + INDEX_ROWS, LANES), jnp.bfloat16),
        in_specs=[vmem] * 4,
        out_specs=vmem,
        compiler_params=limit,
        name="spectra",
    )(arrived, *prepared)
    table = lax.all_to_all(sent, AXES, split_axis=0, concat_axis=0, tiled=True)
    partial = pl.pallas_call(
        functools.partial(cross_kernel, regions, slabs),
        out_shape=jax.ShapeDtypeStruct((devices, LANES // 2, pair_count), jnp.bfloat16),
        in_specs=[vmem],
        out_specs=vmem,
        scratch_shapes=[pltpu.VMEM((regions * LANES, stations), jnp.bfloat16)],
        compiler_params=limit,
        name="cross",
    )(table)
    pieces = lax.all_to_all(partial, AXES, split_axis=0, concat_axis=0, tiled=True)
    return pl.pallas_call(
        place_kernel,
        out_shape=jax.ShapeDtypeStruct((pair_count, 2 * BINS), jnp.bfloat16),
        in_specs=[vmem],
        out_specs=vmem,
        compiler_params=limit,
        name="place",
    )(pieces)


def dft_table():
    sample = jnp.arange(NFFT, dtype=jnp.int32)[:, None]
    frequency = jnp.arange(BINS, dtype=jnp.int32)[None, :]
    phase = (sample * frequency % NFFT).astype(jnp.float32) * (2.0 * math.pi / NFFT)
    return jnp.concatenate([jnp.cos(phase), -jnp.sin(phase)], axis=1).astype(jnp.bfloat16)


def whitened(traces):
    count = traces.shape[0]
    signal = traces.astype(jnp.float32).reshape(count * SEG, NFFT)
    signal = signal - jnp.mean(signal, axis=1, keepdims=True)
    position = jnp.arange(NFFT, dtype=jnp.int32).astype(jnp.float32)
    taper = 0.5 - 0.5 * jnp.cos(position * (2.0 * math.pi / NFFT))
    tapered = (signal * taper[None, :]).astype(jnp.bfloat16)
    spectrum = jnp.dot(tapered, dft_table(), preferred_element_type=jnp.float32)
    real_part = spectrum[:, :BINS]
    imag_part = spectrum[:, BINS:]
    amplitude = jnp.sqrt(real_part * real_part + imag_part * imag_part + 1e-06)
    padded = jnp.pad(amplitude, ((0, 0), (HALF, HALF)))
    smooth = jnp.zeros_like(amplitude)
    for offset in range(2 * HALF + 1):
        smooth = smooth + padded[:, offset : offset + BINS]
    smooth = smooth / (2 * HALF + 1)
    level = jnp.mean(amplitude, axis=1, keepdims=True)
    divisor = smooth + level + 1e-06
    white = spectrum / jnp.concatenate([divisor, divisor], axis=1)
    return white.astype(jnp.bfloat16).reshape(count, SEG * NFFT)


def cross(first_rows, second_rows):
    left = first_rows.astype(jnp.float32).reshape(first_rows.shape[:-1] + (SEG, 2, BINS))
    right = second_rows.astype(jnp.float32).reshape(second_rows.shape[:-1] + (SEG, 2, BINS))
    real_sum = jnp.mean(left[..., 0, :] * right[..., 0, :] + left[..., 1, :] * right[..., 1, :], axis=-2)
    imag_sum = jnp.mean(left[..., 0, :] * right[..., 1, :] - left[..., 1, :] * right[..., 0, :], axis=-2)
    return jnp.concatenate([real_sum, imag_sum], axis=-1).astype(jnp.bfloat16)


def by_rows(records, first_station, second_region, second_station):
    regions = lax.axis_size("region")
    pair_count = first_station.shape[0]
    capacity = max(2, pair_count // regions + pair_count // 16)
    arrived = lax.all_to_all(records, "slab", split_axis=0, concat_axis=1, tiled=True)
    spectra = whitened(arrived)
    width = spectra.shape[1]
    target = second_region[:, 0]
    onehot = (target[:, None] == jnp.arange(regions, dtype=jnp.int32)[None, :]).astype(jnp.int32)
    ranking = jnp.sum((jnp.cumsum(onehot, axis=0) - onehot) * onehot, axis=1)
    slot_index = target * capacity + ranking
    requests = jnp.zeros((regions * capacity,), jnp.int32).at[slot_index].set(second_station).reshape(regions, capacity)
    incoming = lax.all_to_all(requests, "region", split_axis=0, concat_axis=0, tiled=True)
    wanted = jnp.concatenate([first_station, incoming.reshape(-1)])
    piece = lax.all_gather(spectra, "slab", axis=0, tiled=True)
    picked = jnp.take(piece, wanted, axis=0)
    first_rows = picked[:pair_count]
    served = picked[pair_count:]
    returned = lax.all_to_all(
        served.reshape(regions, capacity, width), "region", split_axis=0, concat_axis=0, tiled=True
    )
    second_rows = jnp.take(returned.reshape(regions * capacity, width), slot_index, axis=0)
    return cross(first_rows, second_rows)


def local(records, first_station, second_region, second_station):
    devices = lax.axis_size("region") * lax.axis_size("slab")
    fits = 2 * SEG * BINS == LANES * devices and records.shape[0] <= EXACT and first_station.shape[0] == LANES
    plan = by_bins if fits else by_rows
    return plan(records, first_station, second_region, second_station)


def solution(mesh):
    placed = (
        P(AXES[0], AXES[1]),
        P(AXES),
        P(AXES, None),
        P(AXES),
    )
    return jax.shard_map(local, mesh=mesh, in_specs=placed, out_specs=P(AXES, None), check_vma=False)
```

```python
import functools
import math

import jax
import jax.numpy as jnp
import numpy as np
from jax import lax
from jax.experimental import pallas as pl
from jax.experimental.pallas import tpu as pltpu
from jax.sharding import PartitionSpec as P

NFFT = 2048
BINS = 1024
SEG = 2
HALF = 4
LANES = 128
INDEX_ROWS = 8
RADIX = 16
SMALL_ROWS = 40
EXACT = 256
AXES = ("region", "slab")


def constant_rows():
    fine = np.arange(LANES, dtype=np.int64)
    twiddle = np.arange(RADIX // 2 + 1)[:, None] * fine[None, :] * (2.0 * math.pi / NFFT)
    position = np.arange(NFFT, dtype=np.float64).reshape(RADIX, LANES)
    taper = 0.5 - 0.5 * np.cos(position * (2.0 * math.pi / NFFT))
    mirrored = fine >= LANES // 2
    frequency = np.where(mirrored, LANES - 1 - (fine - LANES // 2), fine)
    phase = (fine[:, None] * frequency[None, :] % LANES) * (2.0 * math.pi / LANES)
    sign = np.where(mirrored, -1.0, 1.0)
    real_side = np.concatenate([np.cos(phase), np.sin(phase)], axis=0)
    imag_side = np.concatenate([-np.sin(phase) * sign, np.cos(phase) * sign], axis=0)
    matrix = np.concatenate([real_side, imag_side], axis=0).astype(jnp.bfloat16)
    small = np.concatenate([np.cos(twiddle), np.sin(twiddle), taper], axis=0)
    small = np.pad(small, ((0, SMALL_ROWS - small.shape[0]), (0, 0)))
    return np.concatenate([small, matrix.astype(np.float64)], axis=0).astype(np.float32)


def prepare_kernel(index_in_ref, rows_ref, index_ref, small_ref, matrix_ref):
    index_ref[...] = index_in_ref[...]
    small_ref[...] = rows_ref[:SMALL_ROWS, :]
    for side in (0, 1):
        at = SMALL_ROWS + side * 2 * LANES
        matrix_ref[:, side * LANES : (side + 1) * LANES] = rows_ref[at : at + 2 * LANES, :].astype(jnp.bfloat16)


def divide_kernel(records_ref, *refs):
    parts = len(refs) - 1
    targets, sem = refs[:-1], refs[-1]
    rows = targets[0].shape[0]
    own = lax.rem(lax.axis_index("slab"), parts)
    copies = []
    for k, target in enumerate(targets):
        block = jnp.bitwise_xor(own, k)
        source = records_ref.at[pl.ds(pl.multiple_of(block * rows, rows), rows), :]
        copies.append(pltpu.make_async_copy(source, target, sem.at[k]))
    for copy in copies:
        copy.start()
    for copy in copies:
        copy.wait()


def short_dft(pieces):
    half = RADIX // 2
    a = [pieces[j] + pieces[j + half] for j in range(half)]
    b = [pieces[j] - pieces[j + half] for j in range(half)]
    f = [a[j] + a[j + 4] for j in range(4)]
    g = [a[j] - a[j + 4] for j in range(4)]
    out = [None] * (half + 1)
    even, odd = f[0] + f[2], f[1] + f[3]
    root = math.sqrt(0.5)
    minus, plus = root * (g[1] - g[3]), root * (g[1] + g[3])
    out[0], out[8] = (even + odd, None), (even - odd, None)
    out[4] = (f[0] - f[2], f[3] - f[1])
    out[2] = (g[0] + minus, -(g[2] + plus))
    out[6] = (g[0] - minus, g[2] - plus)
    d = {j: b[j] - b[half - j] for j in (1, 2, 3)}
    e = {j: b[j] + b[half - j] for j in (1, 2, 3)}
    for k in (1, 3, 5, 7):
        real_part, imag_part = b[0], (-b[4] if k % 4 == 1 else b[4])
        for j in (1, 2, 3):
            real_part = real_part + d[j] * math.cos(math.pi * j * k / half)
            imag_part = imag_part - e[j] * math.sin(math.pi * j * k / half)
        out[k] = (real_part, imag_part)
    return out


def smoothed(size, lane):
    left = lane < LANES // 2
    inside = (lane > 0) & (lane < LANES - 1)

    def turned(values, by):
        return pltpu.roll(values, by, 1)

    line = {t: size[t] for t in range(1, 8)}
    line[0] = jnp.where(left, size[0], jnp.where(inside, turned(size[0], LANES // 2 - 1), 0.0))
    line[8] = jnp.where(left, turned(size[0], LANES // 2), size[0])
    for i in range(1, HALF + 1):
        line[8 + i] = turned(size[8 - i], LANES // 2)
        wrapped = jnp.where(left, turned(size[i], LANES // 2 + 1), turned(size[i], LANES // 2 - 1))
        line[-i] = jnp.where(inside, wrapped, 0.0)
    two = {t: line[t] + line[t + 1] for t in range(-HALF, 8 + HALF)}
    four = {t: two[t] + two[t + 2] for t in range(-HALF, 8 + HALF - 2)}
    nine = [four[t - 4] + four[t] + line[t + 4] for t in range(0, 9)]
    return [jnp.where(left, nine[0], nine[8])] + nine[1:8]


def spectra_kernel(*refs):
    parts = len(refs) - 4
    index_ref, small_ref, matrix_ref, out_ref = refs[parts:]
    rows, samples = refs[0].shape
    count = rows // 2
    own = lax.rem(lax.axis_index("slab"), parts)
    blocks = [ref[...] for ref in refs[:parts]]
    for bit in range(parts.bit_length() - 1):
        swapped = jnp.bitwise_and(jnp.right_shift(own, bit), 1) == 1
        blocks = [jnp.where(swapped, blocks[k ^ (1 << bit)], blocks[k]) for k in range(parts)]
    pieces = []
    for block in blocks:
        block = block.astype(jnp.float32)
        pieces += [block[:, i * LANES : (i + 1) * LANES] for i in range(samples // LANES)]
    total = pieces[0]
    for piece in pieces[1:]:
        total = total + piece
    mean = jnp.sum(total, axis=1, keepdims=True) * (1.0 / NFFT)
    taper = 2 * (RADIX // 2 + 1)
    pieces = [(piece - mean) * small_ref[taper + n1 : taper + n1 + 1, :] for n1, piece in enumerate(pieces)]
    turned = []
    for k1, (real_part, imag_part) in enumerate(short_dft(pieces)):
        cosine = small_ref[k1 : k1 + 1, :]
        sine = small_ref[RADIX // 2 + 1 + k1 : RADIX // 2 + 2 + k1, :]
        if imag_part is None:
            both = [real_part * cosine, -real_part * sine]
        else:
            both = [real_part * cosine + imag_part * sine, imag_part * cosine - real_part * sine]
        turned.append(jnp.concatenate([part.astype(jnp.bfloat16) for part in both], axis=1))
    spectrum = jnp.dot(jnp.concatenate(turned, axis=0), matrix_ref[...], preferred_element_type=jnp.float32)
    lane = lax.broadcasted_iota(jnp.int32, (rows, LANES), 1)
    real_parts, imag_parts = (
        [spectrum[k1 * rows : (k1 + 1) * rows, side * LANES : (side + 1) * LANES] for k1 in range(RADIX // 2 + 1)]
        for side in (0, 1)
    )
    real_parts = [jnp.where(lane < LANES // 2, real_parts[0], real_parts[8])] + real_parts[1:8]
    imag_parts = [jnp.where(lane < LANES // 2, imag_parts[0], imag_parts[8])] + imag_parts[1:8]
    size = [jnp.sqrt(re * re + im * im + 1e-06) for re, im in zip(real_parts, imag_parts)]
    total = size[0]
    for part in size[1:]:
        total = total + part
    level = jnp.sum(total, axis=1, keepdims=True) * (1.0 / BINS) + 1e-06
    group = LANES // 4
    lane_group = lane[:count] // group
    for s, smooth in enumerate(smoothed(size, lane)):
        scale = 1.0 / (smooth * (1.0 / (2 * HALF + 1)) + level)
        white = [real_parts[s] * scale, imag_parts[s] * scale]
        sources = [part[half * count : (half + 1) * count] for half in (0, 1) for part in white]
        for q in range(4):
            block = None
            for place, source in enumerate(sources):
                turn = (place - q) * group % LANES
                moved = pltpu.roll(source, turn, 1) if turn else source
                block = moved if block is None else jnp.where(lane_group == place, moved, block)
            out_ref[4 * s + q, :count, :] = block.astype(jnp.bfloat16)
    for dest in range(out_ref.shape[0]):
        out_ref[dest, count:, :] = index_ref[...]


def cross_kernel(regions, slabs, table_ref, out_ref, flipped_ref):
    devices, rows, _ = table_ref.shape
    count = rows - INDEX_ROWS
    parts = slabs // SEG
    wide = parts * count
    stations = 2 * wide
    bins = LANES // 4
    per_step = 2
    for region in range(regions):
        for segment in range(SEG):
            first_source = region * slabs + segment * parts
            block = table_ref[first_source : first_source + parts, :count, :].reshape(wide, LANES).T
            at = region * LANES + segment * 2 * bins
            for half in (0, 1):
                flipped_ref[at : at + 2 * bins, half * wide : (half + 1) * wide] = block[half * 2 * bins : (half + 1) * 2 * bins]
    column = lax.broadcasted_iota(jnp.int32, (stations, per_step * LANES), 0)
    half, part = column // wide, column % wide // count
    station = (part * 2 + half) * count + column % count
    station = station.astype(jnp.float32).astype(jnp.bfloat16)
    one, zero = jnp.ones((), jnp.bfloat16), jnp.zeros((), jnp.bfloat16)
    for first_device in range(0, devices, per_step):
        named = [table_ref[first_device + k, count:, :] for k in range(per_step)]
        named = jnp.concatenate(named, axis=1)
        first, second, target = named[0:1], named[1:2], named[2:3].astype(jnp.float32)
        home = first_device // slabs
        own = flipped_ref[home * LANES : (home + 1) * LANES, :]
        a = jnp.dot(own, jnp.where(station == first, one, zero), preferred_element_type=jnp.float32)
        pick_second = jnp.where(station == second, one, zero)
        b = None
        for region in range(regions):
            rows_of = flipped_ref[region * LANES : (region + 1) * LANES, :]
            candidate = jnp.dot(rows_of, pick_second, preferred_element_type=jnp.float32)
            b = candidate if b is None else jnp.where(target == region, candidate, b)
        real_sum, imag_sum = 0.0, 0.0
        for segment in range(SEG):
            at = 2 * segment * bins
            ar, ai = a[at : at + bins], a[at + bins : at + 2 * bins]
            br, bi = b[at : at + bins], b[at + bins : at + 2 * bins]
            real_sum = real_sum + (ar * br + ai * bi)
            imag_sum = imag_sum + (ar * bi - ai * br)
        real_sum = (real_sum * (1.0 / SEG)).astype(jnp.bfloat16)
        imag_sum = (imag_sum * (1.0 / SEG)).astype(jnp.bfloat16)
        for k in range(per_step):
            out_ref[first_device + k, :bins, :] = real_sum[:, k * LANES : (k + 1) * LANES]
            out_ref[first_device + k, bins:, :] = imag_sum[:, k * LANES : (k + 1) * LANES]


def place_kernel(in_ref, out_ref):
    devices, rows, _ = in_ref.shape
    bins = rows // 2
    fine = LANES // RADIX
    row = lax.broadcasted_iota(jnp.int32, (LANES, LANES), 0)
    lane = lax.broadcasted_iota(jnp.int32, (LANES, LANES), 1)
    slab, side = row // (2 * fine), row // fine % 2
    k1 = jnp.where(side == 0, slab, jnp.where(slab == 0, RADIX // 2, RADIX - slab))
    order = (lane == k1 + RADIX * (row % fine)).astype(jnp.float32).astype(jnp.bfloat16)
    per_slab = devices // (RADIX // 2)
    per_side = per_slab // 2
    for kind in (0, 1):
        for j in range(BINS // LANES):
            group, at = divmod(j * fine, bins)
            at += kind * bins
            picked = [in_ref[u * per_side + group, at : at + fine, :] for u in range(RADIX)]
            block = jnp.concatenate(picked, axis=0).T
            natural = jnp.dot(block, order, preferred_element_type=jnp.float32)
            place = kind * BINS + j * LANES
            out_ref[:, place : place + LANES] = natural.astype(jnp.bfloat16)


def by_bins(records, first_station, second_region, second_station):
    regions, slabs = lax.axis_size("region"), lax.axis_size("slab")
    devices = regions * slabs
    stations, samples = records.shape
    parts = slabs // SEG
    rows = stations // parts
    count = rows // 2
    pair_count = first_station.shape[0]
    vmem = pl.BlockSpec(memory_space=pltpu.VMEM)
    limit = pltpu.CompilerParams(vmem_limit_bytes=12 << 20)
    divided = pl.pallas_call(
        divide_kernel,
        out_shape=[jax.ShapeDtypeStruct((rows, samples), records.dtype)] * parts,
        in_specs=[pl.BlockSpec(memory_space=pl.ANY)],
        out_specs=[vmem] * parts,
        scratch_shapes=[pltpu.SemaphoreType.DMA((parts,))],
        compiler_params=limit,
        name="divide",
    )(records)
    arrived = [divided[0]] + [
        lax.ppermute(divided[k], "slab", [(i, i ^ k) for i in range(slabs)]) for k in range(1, parts)
    ]
    named = jnp.stack([first_station, second_station, second_region.reshape(-1)])
    index = jnp.pad(named, ((0, INDEX_ROWS - 3), (0, 0))).astype(jnp.bfloat16)
    prepared = pl.pallas_call(
        prepare_kernel,
        out_shape=[
            jax.ShapeDtypeStruct(index.shape, jnp.bfloat16),
            jax.ShapeDtypeStruct((SMALL_ROWS, LANES), jnp.float32),
            jax.ShapeDtypeStruct((2 * LANES, 2 * LANES), jnp.bfloat16),
        ],
        in_specs=[vmem] * 2,
        out_specs=[vmem] * 3,
        compiler_params=limit,
        cost_estimate=pl.CostEstimate(flops=NFFT * BINS, bytes_accessed=NFFT * BINS, transcendentals=0),
        name="prepare",
    )(index, jnp.asarray(constant_rows()))
    sent = pl.pallas_call(
        spectra_kernel,
        out_shape=jax.ShapeDtypeStruct((devices, count + INDEX_ROWS, LANES), jnp.bfloat16),
        in_specs=[vmem] * (parts + 3),
        out_specs=vmem,
        compiler_params=limit,
        name="spectra",
    )(*arrived, *prepared)
    table = lax.all_to_all(sent, AXES, split_axis=0, concat_axis=0, tiled=True)
    partial = pl.pallas_call(
        functools.partial(cross_kernel, regions, slabs),
        out_shape=jax.ShapeDtypeStruct((devices, LANES // 2, pair_count), jnp.bfloat16),
        in_specs=[vmem],
        out_specs=vmem,
        scratch_shapes=[pltpu.VMEM((regions * LANES, stations), jnp.bfloat16)],
        compiler_params=limit,
        name="cross",
    )(table)
    pieces = lax.all_to_all(partial, AXES, split_axis=0, concat_axis=0, tiled=True)
    return pl.pallas_call(
        place_kernel,
        out_shape=jax.ShapeDtypeStruct((pair_count, 2 * BINS), jnp.bfloat16),
        in_specs=[vmem],
        out_specs=vmem,
        compiler_params=limit,
        name="place",
    )(pieces)


def dft_table():
    sample = jnp.arange(NFFT, dtype=jnp.int32)[:, None]
    frequency = jnp.arange(BINS, dtype=jnp.int32)[None, :]
    phase = (sample * frequency % NFFT).astype(jnp.float32) * (2.0 * math.pi / NFFT)
    return jnp.concatenate([jnp.cos(phase), -jnp.sin(phase)], axis=1).astype(jnp.bfloat16)


def whitened(traces):
    count = traces.shape[0]
    signal = traces.astype(jnp.float32).reshape(count * SEG, NFFT)
    signal = signal - jnp.mean(signal, axis=1, keepdims=True)
    position = jnp.arange(NFFT, dtype=jnp.int32).astype(jnp.float32)
    taper = 0.5 - 0.5 * jnp.cos(position * (2.0 * math.pi / NFFT))
    tapered = (signal * taper[None, :]).astype(jnp.bfloat16)
    spectrum = jnp.dot(tapered, dft_table(), preferred_element_type=jnp.float32)
    real_part = spectrum[:, :BINS]
    imag_part = spectrum[:, BINS:]
    amplitude = jnp.sqrt(real_part * real_part + imag_part * imag_part + 1e-06)
    padded = jnp.pad(amplitude, ((0, 0), (HALF, HALF)))
    smooth = jnp.zeros_like(amplitude)
    for offset in range(2 * HALF + 1):
        smooth = smooth + padded[:, offset : offset + BINS]
    smooth = smooth / (2 * HALF + 1)
    level = jnp.mean(amplitude, axis=1, keepdims=True)
    divisor = smooth + level + 1e-06
    white = spectrum / jnp.concatenate([divisor, divisor], axis=1)
    return white.astype(jnp.bfloat16).reshape(count, SEG * NFFT)


def cross(first_rows, second_rows):
    left = first_rows.astype(jnp.float32).reshape(first_rows.shape[:-1] + (SEG, 2, BINS))
    right = second_rows.astype(jnp.float32).reshape(second_rows.shape[:-1] + (SEG, 2, BINS))
    real_sum = jnp.mean(left[..., 0, :] * right[..., 0, :] + left[..., 1, :] * right[..., 1, :], axis=-2)
    imag_sum = jnp.mean(left[..., 0, :] * right[..., 1, :] - left[..., 1, :] * right[..., 0, :], axis=-2)
    return jnp.concatenate([real_sum, imag_sum], axis=-1).astype(jnp.bfloat16)


def by_rows(records, first_station, second_region, second_station):
    regions = lax.axis_size("region")
    pair_count = first_station.shape[0]
    capacity = max(2, pair_count // regions + pair_count // 16)
    arrived = lax.all_to_all(records, "slab", split_axis=0, concat_axis=1, tiled=True)
    spectra = whitened(arrived)
    width = spectra.shape[1]
    target = second_region[:, 0]
    onehot = (target[:, None] == jnp.arange(regions, dtype=jnp.int32)[None, :]).astype(jnp.int32)
    ranking = jnp.sum((jnp.cumsum(onehot, axis=0) - onehot) * onehot, axis=1)
    slot_index = target * capacity + ranking
    requests = jnp.zeros((regions * capacity,), jnp.int32).at[slot_index].set(second_station).reshape(regions, capacity)
    incoming = lax.all_to_all(requests, "region", split_axis=0, concat_axis=0, tiled=True)
    wanted = jnp.concatenate([first_station, incoming.reshape(-1)])
    piece = lax.all_gather(spectra, "slab", axis=0, tiled=True)
    picked = jnp.take(piece, wanted, axis=0)
    first_rows = picked[:pair_count]
    served = picked[pair_count:]
    returned = lax.all_to_all(
        served.reshape(regions, capacity, width), "region", split_axis=0, concat_axis=0, tiled=True
    )
    second_rows = jnp.take(returned.reshape(regions * capacity, width), slot_index, axis=0)
    return cross(first_rows, second_rows)


def local(records, first_station, second_region, second_station):
    slabs = lax.axis_size("slab")
    devices = lax.axis_size("region") * slabs
    fits = (
        devices * LANES == 4 * BINS
        and records.shape == (EXACT, NFFT * SEG // slabs)
        and slabs == 4 * SEG
        and first_station.shape[0] == LANES
    )
    plan = by_bins if fits else by_rows
    return plan(records, first_station, second_region, second_station)


def solution(mesh):
    placed = (
        P(AXES[0], AXES[1]),
        P(AXES),
        P(AXES, None),
        P(AXES),
    )
    return jax.shard_map(local, mesh=mesh, in_specs=placed, out_specs=P(AXES, None), check_vma=False)
```

```python
import functools
import math

import jax
import jax.numpy as jnp
import numpy as np
from jax import lax
from jax.experimental import pallas as pl
from jax.experimental.pallas import tpu as pltpu
from jax.sharding import PartitionSpec as P

NFFT = 2048
BINS = 1024
SEG = 2
HALF = 4
LANES = 128
INDEX_ROWS = 4
RADIX = 16
SMALL_ROWS = 40
EXACT = 256
AXES = ("region", "slab")
RANKS = ("slab", "region")


def constant_rows():
    fine = np.arange(LANES, dtype=np.int64)
    twiddle = np.arange(RADIX // 2 + 1)[:, None] * fine[None, :] * (2.0 * math.pi / NFFT)
    position = np.arange(NFFT, dtype=np.float64).reshape(RADIX, LANES)
    taper = 0.5 - 0.5 * np.cos(position * (2.0 * math.pi / NFFT))
    mirrored = fine >= LANES // 2
    frequency = np.where(mirrored, LANES - 1 - (fine - LANES // 2), fine)
    phase = (fine[:, None] * frequency[None, :] % LANES) * (2.0 * math.pi / LANES)
    sign = np.where(mirrored, -1.0, 1.0)
    real_side = np.concatenate([np.cos(phase), np.sin(phase)], axis=0)
    imag_side = np.concatenate([-np.sin(phase) * sign, np.cos(phase) * sign], axis=0)
    matrix = np.concatenate([real_side, imag_side], axis=0).astype(jnp.bfloat16)
    small = np.concatenate([np.cos(twiddle), np.sin(twiddle), taper], axis=0)
    small = np.pad(small, ((0, SMALL_ROWS - small.shape[0]), (0, 0)))
    return np.concatenate([small, matrix.astype(np.float64)], axis=0).astype(np.float32)


def prepare_kernel(index_in_ref, rows_ref, index_ref, small_ref, matrix_ref):
    index_ref[...] = index_in_ref[...]
    small_ref[...] = rows_ref[:SMALL_ROWS, :]
    for side in (0, 1):
        at = SMALL_ROWS + side * 2 * LANES
        matrix_ref[:, side * LANES : (side + 1) * LANES] = rows_ref[at : at + 2 * LANES, :].astype(jnp.bfloat16)


def divide_kernel(records_ref, *targets):
    parts = len(targets)
    rows = targets[0].shape[0]
    own = lax.rem(lax.axis_index("slab"), parts)
    for k, target in enumerate(targets):
        first = pl.multiple_of(jnp.bitwise_xor(own, k) * rows, rows)
        target[...] = records_ref[pl.ds(first, rows), :]


def short_dft(pieces):
    half = RADIX // 2
    a = [pieces[j] + pieces[j + half] for j in range(half)]
    b = [pieces[j] - pieces[j + half] for j in range(half)]
    f = [a[j] + a[j + 4] for j in range(4)]
    g = [a[j] - a[j + 4] for j in range(4)]
    out = [None] * (half + 1)
    even, odd = f[0] + f[2], f[1] + f[3]
    root = math.sqrt(0.5)
    minus, plus = root * (g[1] - g[3]), root * (g[1] + g[3])
    out[0], out[8] = (even + odd, None), (even - odd, None)
    out[4] = (f[0] - f[2], f[3] - f[1])
    out[2] = (g[0] + minus, -(g[2] + plus))
    out[6] = (g[0] - minus, g[2] - plus)
    d = {j: b[j] - b[half - j] for j in (1, 2, 3)}
    e = {j: b[j] + b[half - j] for j in (1, 2, 3)}
    for k in (1, 3, 5, 7):
        real_part, imag_part = b[0], (-b[4] if k % 4 == 1 else b[4])
        for j in (1, 2, 3):
            real_part = real_part + d[j] * math.cos(math.pi * j * k / half)
            imag_part = imag_part - e[j] * math.sin(math.pi * j * k / half)
        out[k] = (real_part, imag_part)
    return out


def smoothed(size, lane):
    left = lane < LANES // 2
    inside = (lane > 0) & (lane < LANES - 1)

    def turned(values, by):
        return pltpu.roll(values, by, 1)

    line = {t: size[t] for t in range(1, 8)}
    line[0] = jnp.where(left, size[0], jnp.where(inside, turned(size[0], LANES // 2 - 1), 0.0))
    line[8] = jnp.where(left, turned(size[0], LANES // 2), size[0])
    for i in range(1, HALF + 1):
        line[8 + i] = turned(size[8 - i], LANES // 2)
        wrapped = jnp.where(left, turned(size[i], LANES // 2 + 1), turned(size[i], LANES // 2 - 1))
        line[-i] = jnp.where(inside, wrapped, 0.0)
    two = {t: line[t] + line[t + 1] for t in range(-HALF, 8 + HALF)}
    four = {t: two[t] + two[t + 2] for t in range(-HALF, 8 + HALF - 2)}
    nine = [four[t - 4] + four[t] + line[t + 4] for t in range(0, 9)]
    return [jnp.where(left, nine[0], nine[8])] + nine[1:8]


def spectra_kernel(*refs):
    parts = len(refs) - 4
    index_ref, small_ref, matrix_ref, out_ref = refs[parts:]
    rows, samples = refs[0].shape
    count = rows // 2
    own = lax.rem(lax.axis_index("slab"), parts)
    blocks = [ref[...] for ref in refs[:parts]]
    for bit in range(parts.bit_length() - 1):
        swapped = jnp.bitwise_and(jnp.right_shift(own, bit), 1) == 1
        blocks = [jnp.where(swapped, blocks[k ^ (1 << bit)], blocks[k]) for k in range(parts)]
    pieces = []
    for block in blocks:
        block = block.astype(jnp.float32)
        pieces += [block[:, i * LANES : (i + 1) * LANES] for i in range(samples // LANES)]
    total = pieces[0]
    for piece in pieces[1:]:
        total = total + piece
    mean = jnp.sum(total, axis=1, keepdims=True) * (1.0 / NFFT)
    taper = 2 * (RADIX // 2 + 1)
    pieces = [(piece - mean) * small_ref[taper + n1 : taper + n1 + 1, :] for n1, piece in enumerate(pieces)]
    turned = []
    for k1, (real_part, imag_part) in enumerate(short_dft(pieces)):
        cosine = small_ref[k1 : k1 + 1, :]
        sine = small_ref[RADIX // 2 + 1 + k1 : RADIX // 2 + 2 + k1, :]
        if imag_part is None:
            both = [real_part * cosine, -real_part * sine]
        else:
            both = [real_part * cosine + imag_part * sine, imag_part * cosine - real_part * sine]
        turned.append(jnp.concatenate([part.astype(jnp.bfloat16) for part in both], axis=1))
    spectrum = jnp.dot(jnp.concatenate(turned, axis=0), matrix_ref[...], preferred_element_type=jnp.float32)
    lane = lax.broadcasted_iota(jnp.int32, (rows, LANES), 1)
    real_parts, imag_parts = (
        [spectrum[k1 * rows : (k1 + 1) * rows, side * LANES : (side + 1) * LANES] for k1 in range(RADIX // 2 + 1)]
        for side in (0, 1)
    )
    real_parts = [jnp.where(lane < LANES // 2, real_parts[0], real_parts[8])] + real_parts[1:8]
    imag_parts = [jnp.where(lane < LANES // 2, imag_parts[0], imag_parts[8])] + imag_parts[1:8]
    size = [jnp.sqrt(re * re + im * im + 1e-06) for re, im in zip(real_parts, imag_parts)]
    total = size[0]
    for part in size[1:]:
        total = total + part
    level = jnp.sum(total, axis=1, keepdims=True) * (1.0 / BINS) + 1e-06
    group = LANES // 4
    lane_group = lane[:count] // group
    for s, smooth in enumerate(smoothed(size, lane)):
        scale = 1.0 / (smooth * (1.0 / (2 * HALF + 1)) + level)
        white = [real_parts[s] * scale, imag_parts[s] * scale]
        sources = [part[half * count : (half + 1) * count] for half in (0, 1) for part in white]
        for q in range(4):
            block = None
            for place, source in enumerate(sources):
                turn = (place - q) * group % LANES
                moved = pltpu.roll(source, turn, 1) if turn else source
                block = moved if block is None else jnp.where(lane_group == place, moved, block)
            at = (4 * s + q) * (count + INDEX_ROWS)
            out_ref[at : at + count, :] = block.astype(jnp.bfloat16)
            out_ref[at + count : at + count + INDEX_ROWS, :] = index_ref[...]


def cross_kernel(regions, slabs, table_ref, out_ref, flipped_ref):
    devices = regions * slabs
    rows = table_ref.shape[0] // devices
    count = rows - INDEX_ROWS
    parts = slabs // SEG
    wide = parts * count
    stations = 2 * wide
    bins = LANES // 4
    per_step = 2
    for region in range(regions):
        for segment in range(SEG):
            sources = [((segment * parts + part) * regions + region) * rows for part in range(parts)]
            block = jnp.concatenate([table_ref[at : at + count, :] for at in sources], axis=0).T
            at = region * LANES + segment * 2 * bins
            for half in (0, 1):
                flipped_ref[at : at + 2 * bins, half * wide : (half + 1) * wide] = block[half * 2 * bins : (half + 1) * 2 * bins]
    column = lax.broadcasted_iota(jnp.int32, (stations, per_step * LANES), 0)
    half, part = column // wide, column % wide // count
    station = (part * 2 + half) * count + column % count
    station = station.astype(jnp.float32).astype(jnp.bfloat16)
    one, zero = jnp.ones((), jnp.bfloat16), jnp.zeros((), jnp.bfloat16)
    for i in range(devices // per_step):
        home, first_slab = i % regions, i // regions * per_step
        owners = [(first_slab + k) * regions + home for k in range(per_step)]
        named = [table_ref[owner * rows + count : (owner + 1) * rows, :] for owner in owners]
        named = jnp.concatenate(named, axis=1)
        first, second, target = named[0:1], named[1:2], named[2:3].astype(jnp.float32)
        own = flipped_ref[home * LANES : (home + 1) * LANES, :]
        a = jnp.dot(own, jnp.where(station == first, one, zero), preferred_element_type=jnp.float32)
        pick_second = jnp.where(station == second, one, zero)
        b = None
        for region in range(regions):
            rows_of = flipped_ref[region * LANES : (region + 1) * LANES, :]
            candidate = jnp.dot(rows_of, pick_second, preferred_element_type=jnp.float32)
            b = candidate if b is None else jnp.where(target == region, candidate, b)
        real_sum, imag_sum = 0.0, 0.0
        for segment in range(SEG):
            at = 2 * segment * bins
            ar, ai = a[at : at + bins], a[at + bins : at + 2 * bins]
            br, bi = b[at : at + bins], b[at + bins : at + 2 * bins]
            real_sum = real_sum + (ar * br + ai * bi)
            imag_sum = imag_sum + (ar * bi - ai * br)
        real_sum = (real_sum * (1.0 / SEG)).astype(jnp.bfloat16)
        imag_sum = (imag_sum * (1.0 / SEG)).astype(jnp.bfloat16)
        for k, owner in enumerate(owners):
            out_ref[owner, :bins, :] = real_sum[:, k * LANES : (k + 1) * LANES]
            out_ref[owner, bins:, :] = imag_sum[:, k * LANES : (k + 1) * LANES]


def place_kernel(in_ref, out_ref):
    devices, rows, _ = in_ref.shape
    bins = rows // 2
    fine = LANES // RADIX
    row = lax.broadcasted_iota(jnp.int32, (LANES, LANES), 0)
    lane = lax.broadcasted_iota(jnp.int32, (LANES, LANES), 1)
    slab, side = row // (2 * fine), row // fine % 2
    k1 = jnp.where(side == 0, slab, jnp.where(slab == 0, RADIX // 2, RADIX - slab))
    order = (lane == k1 + RADIX * (row % fine)).astype(jnp.float32).astype(jnp.bfloat16)
    per_slab = devices // (RADIX // 2)
    per_side = per_slab // 2
    for kind in (0, 1):
        for j in range(BINS // LANES):
            group, at = divmod(j * fine, bins)
            at += kind * bins
            picked = [in_ref[u * per_side + group, at : at + fine, :] for u in range(RADIX)]
            block = jnp.concatenate(picked, axis=0).T
            natural = jnp.dot(block, order, preferred_element_type=jnp.float32)
            place = kind * BINS + j * LANES
            out_ref[:, place : place + LANES] = natural.astype(jnp.bfloat16)


def by_bins(records, first_station, second_region, second_station):
    regions, slabs = lax.axis_size("region"), lax.axis_size("slab")
    devices = regions * slabs
    stations, samples = records.shape
    parts = slabs // SEG
    rows = stations // parts
    count = rows // 2
    pair_count = first_station.shape[0]
    vmem = pl.BlockSpec(memory_space=pltpu.VMEM)
    limit = pltpu.CompilerParams(vmem_limit_bytes=12 << 20)
    divided = pl.pallas_call(
        divide_kernel,
        out_shape=[jax.ShapeDtypeStruct((rows, samples), records.dtype)] * parts,
        in_specs=[vmem],
        out_specs=[vmem] * parts,
        compiler_params=limit,
        name="divide",
    )(records)
    arrived = list(divided)
    for k in range(parts - 1, 0, -1):
        arrived[k] = lax.ppermute(divided[k], "slab", [(i, i ^ k) for i in range(slabs)])
    named = jnp.stack([first_station, second_station, second_region.reshape(-1)])
    index = jnp.pad(named, ((0, INDEX_ROWS - 3), (0, 0))).astype(jnp.bfloat16)
    prepared = pl.pallas_call(
        prepare_kernel,
        out_shape=[
            jax.ShapeDtypeStruct(index.shape, jnp.bfloat16),
            jax.ShapeDtypeStruct((SMALL_ROWS, LANES), jnp.float32),
            jax.ShapeDtypeStruct((2 * LANES, 2 * LANES), jnp.bfloat16),
        ],
        in_specs=[vmem] * 2,
        out_specs=[vmem] * 3,
        compiler_params=limit,
        cost_estimate=pl.CostEstimate(flops=NFFT * BINS, bytes_accessed=NFFT * BINS, transcendentals=0),
        name="prepare",
    )(index, jnp.asarray(constant_rows()))
    sent = pl.pallas_call(
        spectra_kernel,
        out_shape=jax.ShapeDtypeStruct((devices * (count + INDEX_ROWS), LANES), jnp.bfloat16),
        in_specs=[vmem] * (parts + 3),
        out_specs=vmem,
        compiler_params=limit,
        name="spectra",
    )(*arrived, *prepared)
    blocks = sent.reshape(devices, (count + INDEX_ROWS) // INDEX_ROWS, INDEX_ROWS, LANES)
    table = lax.all_to_all(blocks, RANKS, split_axis=0, concat_axis=0, tiled=True).reshape(sent.shape)
    partial = pl.pallas_call(
        functools.partial(cross_kernel, regions, slabs),
        out_shape=jax.ShapeDtypeStruct((devices, LANES // 2, pair_count), jnp.bfloat16),
        in_specs=[vmem],
        out_specs=vmem,
        scratch_shapes=[pltpu.VMEM((regions * LANES, stations), jnp.bfloat16)],
        compiler_params=limit,
        name="cross",
    )(table)
    pieces = lax.all_to_all(partial, RANKS, split_axis=0, concat_axis=0, tiled=True)
    return pl.pallas_call(
        place_kernel,
        out_shape=jax.ShapeDtypeStruct((pair_count, 2 * BINS), jnp.bfloat16),
        in_specs=[vmem],
        out_specs=vmem,
        compiler_params=limit,
        name="place",
    )(pieces)


def dft_table():
    sample = jnp.arange(NFFT, dtype=jnp.int32)[:, None]
    frequency = jnp.arange(BINS, dtype=jnp.int32)[None, :]
    phase = (sample * frequency % NFFT).astype(jnp.float32) * (2.0 * math.pi / NFFT)
    return jnp.concatenate([jnp.cos(phase), -jnp.sin(phase)], axis=1).astype(jnp.bfloat16)


def whitened(traces):
    count = traces.shape[0]
    signal = traces.astype(jnp.float32).reshape(count * SEG, NFFT)
    signal = signal - jnp.mean(signal, axis=1, keepdims=True)
    position = jnp.arange(NFFT, dtype=jnp.int32).astype(jnp.float32)
    taper = 0.5 - 0.5 * jnp.cos(position * (2.0 * math.pi / NFFT))
    tapered = (signal * taper[None, :]).astype(jnp.bfloat16)
    spectrum = jnp.dot(tapered, dft_table(), preferred_element_type=jnp.float32)
    real_part = spectrum[:, :BINS]
    imag_part = spectrum[:, BINS:]
    amplitude = jnp.sqrt(real_part * real_part + imag_part * imag_part + 1e-06)
    padded = jnp.pad(amplitude, ((0, 0), (HALF, HALF)))
    smooth = jnp.zeros_like(amplitude)
    for offset in range(2 * HALF + 1):
        smooth = smooth + padded[:, offset : offset + BINS]
    smooth = smooth / (2 * HALF + 1)
    level = jnp.mean(amplitude, axis=1, keepdims=True)
    divisor = smooth + level + 1e-06
    white = spectrum / jnp.concatenate([divisor, divisor], axis=1)
    return white.astype(jnp.bfloat16).reshape(count, SEG * NFFT)


def cross(first_rows, second_rows):
    left = first_rows.astype(jnp.float32).reshape(first_rows.shape[:-1] + (SEG, 2, BINS))
    right = second_rows.astype(jnp.float32).reshape(second_rows.shape[:-1] + (SEG, 2, BINS))
    real_sum = jnp.mean(left[..., 0, :] * right[..., 0, :] + left[..., 1, :] * right[..., 1, :], axis=-2)
    imag_sum = jnp.mean(left[..., 0, :] * right[..., 1, :] - left[..., 1, :] * right[..., 0, :], axis=-2)
    return jnp.concatenate([real_sum, imag_sum], axis=-1).astype(jnp.bfloat16)


def by_rows(records, first_station, second_region, second_station):
    regions = lax.axis_size("region")
    pair_count = first_station.shape[0]
    capacity = max(2, pair_count // regions + pair_count // 16)
    arrived = lax.all_to_all(records, "slab", split_axis=0, concat_axis=1, tiled=True)
    spectra = whitened(arrived)
    width = spectra.shape[1]
    target = second_region[:, 0]
    onehot = (target[:, None] == jnp.arange(regions, dtype=jnp.int32)[None, :]).astype(jnp.int32)
    ranking = jnp.sum((jnp.cumsum(onehot, axis=0) - onehot) * onehot, axis=1)
    slot_index = target * capacity + ranking
    requests = jnp.zeros((regions * capacity,), jnp.int32).at[slot_index].set(second_station).reshape(regions, capacity)
    incoming = lax.all_to_all(requests, "region", split_axis=0, concat_axis=0, tiled=True)
    wanted = jnp.concatenate([first_station, incoming.reshape(-1)])
    piece = lax.all_gather(spectra, "slab", axis=0, tiled=True)
    picked = jnp.take(piece, wanted, axis=0)
    first_rows = picked[:pair_count]
    served = picked[pair_count:]
    returned = lax.all_to_all(
        served.reshape(regions, capacity, width), "region", split_axis=0, concat_axis=0, tiled=True
    )
    second_rows = jnp.take(returned.reshape(regions * capacity, width), slot_index, axis=0)
    return cross(first_rows, second_rows)


def local(records, first_station, second_region, second_station):
    slabs = lax.axis_size("slab")
    devices = lax.axis_size("region") * slabs
    fits = (
        devices * LANES == 4 * BINS
        and records.shape == (EXACT, NFFT * SEG // slabs)
        and slabs == 4 * SEG
        and first_station.shape[0] == LANES
    )
    plan = by_bins if fits else by_rows
    return plan(records, first_station, second_region, second_station)


def solution(mesh):
    placed = (
        P(AXES[0], AXES[1]),
        P(AXES),
        P(AXES, None),
        P(AXES),
    )
    return jax.shard_map(local, mesh=mesh, in_specs=placed, out_specs=P(AXES, None), check_vma=False)
```

```python
import functools
import math

import jax
import jax.numpy as jnp
import numpy as np
from jax import lax
from jax.experimental import pallas as pl
from jax.experimental.pallas import tpu as pltpu
from jax.sharding import PartitionSpec as P

NFFT = 2048
BINS = 1024
SEG = 2
HALF = 4
LANES = 128
INDEX_ROWS = 4
CLASSES = 4
WIDTH = BINS // CLASSES
COARSE, FINE = 16, 32
TAPER_ROWS = 8
EXACT = 256
AXES = ("region", "slab")
RANKS = ("slab", "region")


def constant_rows():
    rows = []
    for pair in range(CLASSES // 2):
        frequency = np.concatenate([CLASSES * np.arange(WIDTH, dtype=np.int64) + 2 * pair + side for side in (0, 1)])
        for sample in (FINE * np.arange(COARSE, dtype=np.int64), np.arange(FINE, dtype=np.int64)):
            phase = (sample[:, None] * frequency[None, :] % NFFT) * (2.0 * math.pi / NFFT)
            rows += [np.cos(phase), np.sin(phase)]
    angle = np.arange(NFFT, dtype=np.float32) * np.float32(2.0 * math.pi / NFFT)
    cosine = np.cos(angle.astype(np.float64)).astype(np.float32)
    taper = (np.float32(0.5) - np.float32(0.5) * cosine).reshape(CLASSES, -1)
    rows.append(np.pad(taper, ((0, TAPER_ROWS - CLASSES), (0, 0))))
    return np.concatenate(rows, axis=0).astype(np.float32)


def prepare_kernel(named_ref, rows_ref, index_ref, taper_ref, table_ref):
    row = lax.broadcasted_iota(jnp.int32, index_ref.shape, 0)
    named = lax.rem(jnp.right_shift(named_ref[...], 8 * row), EXACT)
    index_ref[...] = named.astype(jnp.float32).astype(jnp.bfloat16)
    held = 2 * (COARSE + FINE)
    taper_ref[...] = rows_ref[held * CLASSES // 2 :, :]
    for pair in range(CLASSES // 2):
        at = pair * held
        fine_cos = rows_ref[at + 2 * COARSE : at + 2 * COARSE + FINE, :]
        fine_sin = rows_ref[at + 2 * COARSE + FINE : at + held, :]

        def block(i, _):
            coarse_cos = rows_ref[pl.ds(at + i, 1), :]
            coarse_sin = rows_ref[pl.ds(at + COARSE + i, 1), :]
            cosine = (coarse_cos * fine_cos - coarse_sin * fine_sin).astype(jnp.bfloat16)
            sine = (-coarse_sin * fine_cos - coarse_cos * fine_sin).astype(jnp.bfloat16)
            for side in (0, 1):
                first = (2 * pair + side) * FINE * COARSE + i * FINE
                place = pl.ds(pl.multiple_of(first, FINE), FINE)
                table_ref[place, :WIDTH] = cosine[:, side * WIDTH : (side + 1) * WIDTH]
                table_ref[place, WIDTH:] = sine[:, side * WIDTH : (side + 1) * WIDTH]
            return 0

        lax.fori_loop(0, COARSE, block, 0, unroll=4)


def divide_kernel(records_ref, *targets):
    parts = len(targets)
    rows = targets[0].shape[0]
    own = lax.rem(lax.axis_index("slab"), parts)
    for k, target in enumerate(targets):
        first = pl.multiple_of(jnp.bitwise_xor(own, k) * rows, rows)
        target[...] = records_ref[pl.ds(first, rows), :]


def shifted(values, step):
    width = values.shape[1]
    lane = lax.broadcasted_iota(jnp.int32, values.shape, 1)
    moved = pltpu.roll(values, (-step) % width, 1)
    return jnp.where((lane + step >= 0) & (lane + step < width), moved, 0.0)


def two_terms(values):
    coarse = values.astype(jnp.bfloat16)
    fine = (values - coarse.astype(jnp.float32)).astype(jnp.bfloat16)
    return jnp.concatenate([coarse, fine], axis=0)


def spectra_kernel(*refs):
    parts = len(refs) - 4
    index_ref, taper_ref, table_ref, out_ref = refs[parts:]
    rows, samples = refs[0].shape
    count = rows // 2
    own = lax.rem(lax.axis_index("slab"), parts)
    blocks = [ref[...] for ref in refs[:parts]]
    for bit in range(parts.bit_length() - 1):
        swapped = jnp.bitwise_and(jnp.right_shift(own, bit), 1) == 1
        blocks = [jnp.where(swapped, blocks[k ^ (1 << bit)], blocks[k]) for k in range(parts)]
    blocks = [block.astype(jnp.float32) for block in blocks]
    mean = jnp.sum((blocks[0] + blocks[1]) + (blocks[2] + blocks[3]), axis=1, keepdims=True) * (1.0 / NFFT)
    blocks = [((block - mean) * taper_ref[j : j + 1, :]).astype(jnp.bfloat16) for j, block in enumerate(blocks)]
    blocks = [block.astype(jnp.float32) for block in blocks]

    def transformed(values, r):
        table = table_ref[r * samples : (r + 1) * samples, :]
        both = jnp.dot(two_terms(values), table, preferred_element_type=jnp.float32)
        both = both[: values.shape[0]] + both[values.shape[0] :]
        return both[:, :WIDTH], both[:, WIDTH:]

    added, taken = ([blocks[j] + sign * blocks[j + 2] for j in (0, 1)] for sign in (1.0, -1.0))
    spectrum = [None] * CLASSES
    spectrum[0] = transformed(added[0] + added[1], 0)
    spectrum[2] = transformed(added[0] - added[1], 2)
    for r, sign in ((1, 1.0), (3, -1.0)):
        with_cos, with_sin = transformed(jnp.concatenate(taken, axis=0), r)
        spectrum[r] = (with_cos[:rows] + sign * with_sin[rows:], with_sin[:rows] - sign * with_cos[rows:])
    size = [jnp.sqrt(re * re + im * im + 1e-06) for re, im in spectrum]
    every = (size[0] + size[1]) + (size[2] + size[3])
    level = jnp.sum(every, axis=1, keepdims=True) * (1.0 / BINS) + 1e-06
    before, after = ([shifted(part, step) for part in size] for step in (-1, 1))
    group = LANES // 4
    lane_group = lax.broadcasted_iota(jnp.int32, (count, LANES), 1) // group
    for r in range(CLASSES):
        smooth = every
        for part in before[r:] + after[: r + 1]:
            smooth = smooth + part
        scale = 1.0 / (smooth * (1.0 / (2 * HALF + 1)) + level)
        white = [(part * scale).astype(jnp.bfloat16) for part in spectrum[r]]
        for s in range(WIDTH // LANES):
            sources = [
                part[side * count : (side + 1) * count, s * LANES : (s + 1) * LANES] for side in (0, 1) for part in white
            ]
            for q in range(4):
                block = None
                for place, source in enumerate(sources):
                    turn = (place - q) * group % LANES
                    moved = pltpu.roll(source, turn, 1) if turn else source
                    block = moved if block is None else jnp.where(lane_group == place, moved, block)
                at = (r * WIDTH // group + 4 * s + q) * (count + INDEX_ROWS)
                out_ref[at : at + count, :] = block
                out_ref[at + count : at + count + INDEX_ROWS, :] = index_ref[...]


def cross_kernel(regions, slabs, table_ref, out_ref, flipped_ref):
    devices = regions * slabs
    rows = table_ref.shape[0] // devices
    count = rows - INDEX_ROWS
    parts = slabs // SEG
    wide = parts * count
    stations = 2 * wide
    bins = LANES // 4
    per_step = 2
    for region in range(regions):
        for segment in range(SEG):
            sources = [((segment * parts + part) * regions + region) * rows for part in range(parts)]
            block = jnp.concatenate([table_ref[at : at + count, :] for at in sources], axis=0).T
            at = region * LANES + segment * 2 * bins
            for half in (0, 1):
                flipped_ref[at : at + 2 * bins, half * wide : (half + 1) * wide] = block[half * 2 * bins : (half + 1) * 2 * bins]
    column = lax.broadcasted_iota(jnp.int32, (stations, per_step * LANES), 0)
    half, part = column // wide, column % wide // count
    station = (part * 2 + half) * count + column % count
    station = station.astype(jnp.float32).astype(jnp.bfloat16)
    one, zero = jnp.ones((), jnp.bfloat16), jnp.zeros((), jnp.bfloat16)
    for i in range(devices // per_step):
        home, first_slab = i % regions, i // regions * per_step
        owners = [(first_slab + k) * regions + home for k in range(per_step)]
        named = [table_ref[owner * rows + count : (owner + 1) * rows, :] for owner in owners]
        named = jnp.concatenate(named, axis=1)
        first, second, target = named[0:1], named[1:2], named[2:3].astype(jnp.float32)
        own = flipped_ref[home * LANES : (home + 1) * LANES, :]
        a = jnp.dot(own, jnp.where(station == first, one, zero), preferred_element_type=jnp.float32)
        pick_second = jnp.where(station == second, one, zero)
        b = None
        for region in range(regions):
            rows_of = flipped_ref[region * LANES : (region + 1) * LANES, :]
            candidate = jnp.dot(rows_of, pick_second, preferred_element_type=jnp.float32)
            b = candidate if b is None else jnp.where(target == region, candidate, b)
        real_sum, imag_sum = 0.0, 0.0
        for segment in range(SEG):
            at = 2 * segment * bins
            ar, ai = a[at : at + bins], a[at + bins : at + 2 * bins]
            br, bi = b[at : at + bins], b[at + bins : at + 2 * bins]
            real_sum = real_sum + (ar * br + ai * bi)
            imag_sum = imag_sum + (ar * bi - ai * br)
        real_sum = (real_sum * (1.0 / SEG)).astype(jnp.bfloat16)
        imag_sum = (imag_sum * (1.0 / SEG)).astype(jnp.bfloat16)
        for k, owner in enumerate(owners):
            out_ref[owner, :bins, :] = real_sum[:, k * LANES : (k + 1) * LANES]
            out_ref[owner, bins:, :] = imag_sum[:, k * LANES : (k + 1) * LANES]


def place_kernel(in_ref, out_ref):
    devices, rows, _ = in_ref.shape
    bins = rows // 2
    row = lax.broadcasted_iota(jnp.int32, (LANES, LANES), 0)
    lane = lax.broadcasted_iota(jnp.int32, (LANES, LANES), 1)
    order = (lane == CLASSES * (row % bins) + row // bins).astype(jnp.float32).astype(jnp.bfloat16)
    for kind in (0, 1):
        for j in range(devices // CLASSES):
            sources = range(j, devices, devices // CLASSES)
            block = jnp.concatenate([in_ref[u, kind * bins : (kind + 1) * bins, :] for u in sources], axis=0).T
            natural = jnp.dot(block, order, preferred_element_type=jnp.float32)
            place = kind * BINS + j * LANES
            out_ref[:, place : place + LANES] = natural.astype(jnp.bfloat16)


def by_bins(records, first_station, second_region, second_station):
    regions, slabs = lax.axis_size("region"), lax.axis_size("slab")
    devices = regions * slabs
    stations, samples = records.shape
    parts = slabs // SEG
    rows = stations // parts
    count = rows // 2
    pair_count = first_station.shape[0]
    vmem = pl.BlockSpec(memory_space=pltpu.VMEM)
    limit = pltpu.CompilerParams(vmem_limit_bytes=12 << 20)
    divided = pl.pallas_call(
        divide_kernel,
        out_shape=[jax.ShapeDtypeStruct((rows, samples), records.dtype)] * parts,
        in_specs=[vmem],
        out_specs=[vmem] * parts,
        compiler_params=limit,
        name="divide",
    )(records)
    arrived = list(divided)
    for k in range(parts - 1, 0, -1):
        arrived[k] = lax.ppermute(divided[k], "slab", [(i, i ^ k) for i in range(slabs)])
    named = first_station + EXACT * second_station + EXACT * EXACT * second_region.reshape(-1)
    prepared = pl.pallas_call(
        prepare_kernel,
        out_shape=[
            jax.ShapeDtypeStruct((INDEX_ROWS, pair_count), jnp.bfloat16),
            jax.ShapeDtypeStruct((TAPER_ROWS, samples), jnp.float32),
            jax.ShapeDtypeStruct((CLASSES * samples, 2 * WIDTH), jnp.bfloat16),
        ],
        in_specs=[vmem] * 2,
        out_specs=[vmem] * 3,
        compiler_params=limit,
        cost_estimate=pl.CostEstimate(flops=NFFT * BINS, bytes_accessed=NFFT * BINS, transcendentals=0),
        name="prepare",
    )(named.reshape(1, -1), jnp.asarray(constant_rows()))
    sent = pl.pallas_call(
        spectra_kernel,
        out_shape=jax.ShapeDtypeStruct((devices * (count + INDEX_ROWS), LANES), jnp.bfloat16),
        in_specs=[vmem] * (parts + 3),
        out_specs=vmem,
        compiler_params=limit,
        name="spectra",
    )(*arrived, *prepared)
    blocks = sent.reshape(devices, (count + INDEX_ROWS) // INDEX_ROWS, INDEX_ROWS, LANES)
    table = lax.all_to_all(blocks, RANKS, split_axis=0, concat_axis=0, tiled=True).reshape(sent.shape)
    partial = pl.pallas_call(
        functools.partial(cross_kernel, regions, slabs),
        out_shape=jax.ShapeDtypeStruct((devices, LANES // 2, pair_count), jnp.bfloat16),
        in_specs=[vmem],
        out_specs=vmem,
        scratch_shapes=[pltpu.VMEM((regions * LANES, stations), jnp.bfloat16)],
        compiler_params=limit,
        name="cross",
    )(table)
    pieces = lax.all_to_all(partial, RANKS, split_axis=0, concat_axis=0, tiled=True)
    return pl.pallas_call(
        place_kernel,
        out_shape=jax.ShapeDtypeStruct((pair_count, 2 * BINS), jnp.bfloat16),
        in_specs=[vmem],
        out_specs=vmem,
        compiler_params=limit,
        name="place",
    )(pieces)


def dft_table():
    sample = jnp.arange(NFFT, dtype=jnp.int32)[:, None]
    frequency = jnp.arange(BINS, dtype=jnp.int32)[None, :]
    phase = (sample * frequency % NFFT).astype(jnp.float32) * (2.0 * math.pi / NFFT)
    return jnp.concatenate([jnp.cos(phase), -jnp.sin(phase)], axis=1).astype(jnp.bfloat16)


def whitened(traces):
    count = traces.shape[0]
    signal = traces.astype(jnp.float32).reshape(count * SEG, NFFT)
    signal = signal - jnp.mean(signal, axis=1, keepdims=True)
    position = jnp.arange(NFFT, dtype=jnp.int32).astype(jnp.float32)
    taper = 0.5 - 0.5 * jnp.cos(position * (2.0 * math.pi / NFFT))
    tapered = (signal * taper[None, :]).astype(jnp.bfloat16)
    spectrum = jnp.dot(tapered, dft_table(), preferred_element_type=jnp.float32)
    real_part = spectrum[:, :BINS]
    imag_part = spectrum[:, BINS:]
    amplitude = jnp.sqrt(real_part * real_part + imag_part * imag_part + 1e-06)
    padded = jnp.pad(amplitude, ((0, 0), (HALF, HALF)))
    smooth = jnp.zeros_like(amplitude)
    for offset in range(2 * HALF + 1):
        smooth = smooth + padded[:, offset : offset + BINS]
    smooth = smooth / (2 * HALF + 1)
    level = jnp.mean(amplitude, axis=1, keepdims=True)
    divisor = smooth + level + 1e-06
    white = spectrum / jnp.concatenate([divisor, divisor], axis=1)
    return white.astype(jnp.bfloat16).reshape(count, SEG * NFFT)


def cross(first_rows, second_rows):
    left = first_rows.astype(jnp.float32).reshape(first_rows.shape[:-1] + (SEG, 2, BINS))
    right = second_rows.astype(jnp.float32).reshape(second_rows.shape[:-1] + (SEG, 2, BINS))
    real_sum = jnp.mean(left[..., 0, :] * right[..., 0, :] + left[..., 1, :] * right[..., 1, :], axis=-2)
    imag_sum = jnp.mean(left[..., 0, :] * right[..., 1, :] - left[..., 1, :] * right[..., 0, :], axis=-2)
    return jnp.concatenate([real_sum, imag_sum], axis=-1).astype(jnp.bfloat16)


def by_rows(records, first_station, second_region, second_station):
    regions = lax.axis_size("region")
    pair_count = first_station.shape[0]
    capacity = max(2, pair_count // regions + pair_count // 16)
    arrived = lax.all_to_all(records, "slab", split_axis=0, concat_axis=1, tiled=True)
    spectra = whitened(arrived)
    width = spectra.shape[1]
    target = second_region[:, 0]
    onehot = (target[:, None] == jnp.arange(regions, dtype=jnp.int32)[None, :]).astype(jnp.int32)
    ranking = jnp.sum((jnp.cumsum(onehot, axis=0) - onehot) * onehot, axis=1)
    slot_index = target * capacity + ranking
    requests = jnp.zeros((regions * capacity,), jnp.int32).at[slot_index].set(second_station).reshape(regions, capacity)
    incoming = lax.all_to_all(requests, "region", split_axis=0, concat_axis=0, tiled=True)
    wanted = jnp.concatenate([first_station, incoming.reshape(-1)])
    piece = lax.all_gather(spectra, "slab", axis=0, tiled=True)
    picked = jnp.take(piece, wanted, axis=0)
    first_rows = picked[:pair_count]
    served = picked[pair_count:]
    returned = lax.all_to_all(
        served.reshape(regions, capacity, width), "region", split_axis=0, concat_axis=0, tiled=True
    )
    second_rows = jnp.take(returned.reshape(regions * capacity, width), slot_index, axis=0)
    return cross(first_rows, second_rows)


def local(records, first_station, second_region, second_station):
    slabs = lax.axis_size("slab")
    devices = lax.axis_size("region") * slabs
    fits = (
        devices * LANES == 4 * BINS
        and records.shape == (EXACT, NFFT * SEG // slabs)
        and slabs == 4 * SEG
        and first_station.shape[0] == LANES
    )
    plan = by_bins if fits else by_rows
    return plan(records, first_station, second_region, second_station)


def solution(mesh):
    placed = (
        P(AXES[0], AXES[1]),
        P(AXES),
        P(AXES, None),
        P(AXES),
    )
    return jax.shard_map(local, mesh=mesh, in_specs=placed, out_specs=P(AXES, None), check_vma=False)
```

```python
import functools
import math

import jax
import jax.numpy as jnp
import numpy as np
from jax import lax
from jax.experimental import pallas as pl
from jax.experimental.pallas import tpu as pltpu
from jax.sharding import PartitionSpec as P

NFFT = 2048
BINS = 1024
SEG = 2
HALF = 4
LANES = 128
INDEX_ROWS = 4
CLASSES = 4
WIDTH = BINS // CLASSES
COARSE, FINE = 16, 32
TAPER_ROWS = 8
EXACT = 256
AXES = ("region", "slab")
SPECTRA_RANKS = [
    16, 8, 24, 0, 15, 23, 7, 31, 26, 10, 18, 2, 19, 11, 27, 3,
    20, 13, 28, 4, 21, 12, 29, 5, 22, 14, 30, 6, 17, 9, 25, 1,
]
RESULT_RANKS = [
    0, 8, 16, 24, 2, 18, 10, 26, 7, 15, 23, 31, 3, 11, 19, 27,
    4, 12, 20, 28, 17, 13, 21, 29, 6, 14, 22, 30, 1, 9, 5, 25,
]


def constant_rows():
    rows = []
    for pair in range(CLASSES // 2):
        frequency = np.concatenate([CLASSES * np.arange(WIDTH, dtype=np.int64) + 2 * pair + side for side in (0, 1)])
        for sample in (FINE * np.arange(COARSE, dtype=np.int64), np.arange(FINE, dtype=np.int64)):
            phase = (sample[:, None] * frequency[None, :] % NFFT) * (2.0 * math.pi / NFFT)
            rows += [np.cos(phase), np.sin(phase)]
    angle = np.arange(NFFT, dtype=np.float32) * np.float32(2.0 * math.pi / NFFT)
    cosine = np.cos(angle.astype(np.float64)).astype(np.float32)
    taper = (np.float32(0.5) - np.float32(0.5) * cosine).reshape(CLASSES, -1)
    rows.append(np.pad(taper, ((0, TAPER_ROWS - CLASSES), (0, 0))))
    return np.concatenate(rows, axis=0).astype(np.float32)


def prepare_kernel(named_ref, rows_ref, index_ref, taper_ref, table_ref):
    row = lax.broadcasted_iota(jnp.int32, index_ref.shape, 0)
    named = lax.rem(jnp.right_shift(named_ref[...], 8 * row), EXACT)
    index_ref[...] = named.astype(jnp.float32).astype(jnp.bfloat16)
    held = 2 * (COARSE + FINE)
    taper_ref[...] = rows_ref[held * CLASSES // 2 :, :]
    for pair in range(CLASSES // 2):
        at = pair * held
        fine_cos = rows_ref[at + 2 * COARSE : at + 2 * COARSE + FINE, :]
        fine_sin = rows_ref[at + 2 * COARSE + FINE : at + held, :]

        def block(i, _):
            coarse_cos = rows_ref[pl.ds(at + i, 1), :]
            coarse_sin = rows_ref[pl.ds(at + COARSE + i, 1), :]
            cosine = (coarse_cos * fine_cos - coarse_sin * fine_sin).astype(jnp.bfloat16)
            sine = (-coarse_sin * fine_cos - coarse_cos * fine_sin).astype(jnp.bfloat16)
            for side in (0, 1):
                first = (2 * pair + side) * FINE * COARSE + i * FINE
                place = pl.ds(pl.multiple_of(first, FINE), FINE)
                table_ref[place, :WIDTH] = cosine[:, side * WIDTH : (side + 1) * WIDTH]
                table_ref[place, WIDTH:] = sine[:, side * WIDTH : (side + 1) * WIDTH]
            return 0

        lax.fori_loop(0, COARSE, block, 0, unroll=4)


def divide_kernel(records_ref, *targets):
    parts = len(targets)
    rows = targets[0].shape[0]
    own = lax.rem(lax.axis_index("slab"), parts)
    for k, target in enumerate(targets):
        first = pl.multiple_of(jnp.bitwise_xor(own, k) * rows, rows)
        target[...] = records_ref[pl.ds(first, rows), :]


def shifted(values, step):
    width = values.shape[1]
    lane = lax.broadcasted_iota(jnp.int32, values.shape, 1)
    moved = pltpu.roll(values, (-step) % width, 1)
    return jnp.where((lane + step >= 0) & (lane + step < width), moved, 0.0)


def two_terms(values):
    coarse = values.astype(jnp.bfloat16)
    fine = (values - coarse.astype(jnp.float32)).astype(jnp.bfloat16)
    return jnp.concatenate([coarse, fine], axis=0)


def spectra_kernel(*refs):
    parts = len(refs) - 4
    index_ref, taper_ref, table_ref, out_ref = refs[parts:]
    rows, samples = refs[0].shape
    count = rows // 2
    own = lax.rem(lax.axis_index("slab"), parts)
    blocks = [ref[...] for ref in refs[:parts]]
    for bit in range(parts.bit_length() - 1):
        swapped = jnp.bitwise_and(jnp.right_shift(own, bit), 1) == 1
        blocks = [jnp.where(swapped, blocks[k ^ (1 << bit)], blocks[k]) for k in range(parts)]
    blocks = [block.astype(jnp.float32) for block in blocks]
    mean = jnp.sum((blocks[0] + blocks[1]) + (blocks[2] + blocks[3]), axis=1, keepdims=True) * (1.0 / NFFT)
    blocks = [((block - mean) * taper_ref[j : j + 1, :]).astype(jnp.bfloat16) for j, block in enumerate(blocks)]
    blocks = [block.astype(jnp.float32) for block in blocks]

    def transformed(values, r):
        table = table_ref[r * samples : (r + 1) * samples, :]
        both = jnp.dot(two_terms(values), table, preferred_element_type=jnp.float32)
        both = both[: values.shape[0]] + both[values.shape[0] :]
        return both[:, :WIDTH], both[:, WIDTH:]

    added, taken = ([blocks[j] + sign * blocks[j + 2] for j in (0, 1)] for sign in (1.0, -1.0))
    spectrum = [None] * CLASSES
    spectrum[0] = transformed(added[0] + added[1], 0)
    spectrum[2] = transformed(added[0] - added[1], 2)
    for r, sign in ((1, 1.0), (3, -1.0)):
        with_cos, with_sin = transformed(jnp.concatenate(taken, axis=0), r)
        spectrum[r] = (with_cos[:rows] + sign * with_sin[rows:], with_sin[:rows] - sign * with_cos[rows:])
    size = [jnp.sqrt(re * re + im * im + 1e-06) for re, im in spectrum]
    every = (size[0] + size[1]) + (size[2] + size[3])
    level = jnp.sum(every, axis=1, keepdims=True) * (1.0 / BINS) + 1e-06
    before, after = ([shifted(part, step) for part in size] for step in (-1, 1))
    group = LANES // 4
    lane_group = lax.broadcasted_iota(jnp.int32, (count, LANES), 1) // group
    for r in range(CLASSES):
        smooth = every
        for part in before[r:] + after[: r + 1]:
            smooth = smooth + part
        scale = 1.0 / (smooth * (1.0 / (2 * HALF + 1)) + level)
        white = [(part * scale).astype(jnp.bfloat16) for part in spectrum[r]]
        for s in range(WIDTH // LANES):
            sources = [
                part[side * count : (side + 1) * count, s * LANES : (s + 1) * LANES] for side in (0, 1) for part in white
            ]
            for q in range(4):
                block = None
                for place, source in enumerate(sources):
                    turn = (place - q) * group % LANES
                    moved = pltpu.roll(source, turn, 1) if turn else source
                    block = moved if block is None else jnp.where(lane_group == place, moved, block)
                at = (r * WIDTH // group + 4 * s + q) * (count + INDEX_ROWS)
                out_ref[at : at + count, :] = block
                out_ref[at + count : at + count + INDEX_ROWS, :] = index_ref[...]


def cross_kernel(regions, slabs, table_ref, out_ref, flipped_ref):
    devices = regions * slabs
    rows = table_ref.shape[0] // devices
    count = rows - INDEX_ROWS
    parts = slabs // SEG
    wide = parts * count
    stations = 2 * wide
    bins = LANES // 4
    per_step = 2
    for region in range(regions):
        for segment in range(SEG):
            sources = [SPECTRA_RANKS.index(region * slabs + segment * parts + part) * rows for part in range(parts)]
            block = jnp.concatenate([table_ref[at : at + count, :] for at in sources], axis=0).T
            at = region * LANES + segment * 2 * bins
            for half in (0, 1):
                flipped_ref[at : at + 2 * bins, half * wide : (half + 1) * wide] = block[half * 2 * bins : (half + 1) * 2 * bins]
    column = lax.broadcasted_iota(jnp.int32, (stations, per_step * LANES), 0)
    half, part = column // wide, column % wide // count
    station = (part * 2 + half) * count + column % count
    station = station.astype(jnp.float32).astype(jnp.bfloat16)
    one, zero = jnp.ones((), jnp.bfloat16), jnp.zeros((), jnp.bfloat16)
    for i in range(devices // per_step):
        home, first_slab = i % regions, i // regions * per_step
        owners = [home * slabs + first_slab + k for k in range(per_step)]
        places = [SPECTRA_RANKS.index(owner) * rows for owner in owners]
        named = [table_ref[at + count : at + rows, :] for at in places]
        named = jnp.concatenate(named, axis=1)
        first, second, target = named[0:1], named[1:2], named[2:3].astype(jnp.float32)
        own = flipped_ref[home * LANES : (home + 1) * LANES, :]
        a = jnp.dot(own, jnp.where(station == first, one, zero), preferred_element_type=jnp.float32)
        pick_second = jnp.where(station == second, one, zero)
        b = None
        for region in range(regions):
            rows_of = flipped_ref[region * LANES : (region + 1) * LANES, :]
            candidate = jnp.dot(rows_of, pick_second, preferred_element_type=jnp.float32)
            b = candidate if b is None else jnp.where(target == region, candidate, b)
        real_sum, imag_sum = 0.0, 0.0
        for segment in range(SEG):
            at = 2 * segment * bins
            ar, ai = a[at : at + bins], a[at + bins : at + 2 * bins]
            br, bi = b[at : at + bins], b[at + bins : at + 2 * bins]
            real_sum = real_sum + (ar * br + ai * bi)
            imag_sum = imag_sum + (ar * bi - ai * br)
        real_sum = (real_sum * (1.0 / SEG)).astype(jnp.bfloat16)
        imag_sum = (imag_sum * (1.0 / SEG)).astype(jnp.bfloat16)
        for k, owner in enumerate(owners):
            at = RESULT_RANKS.index(owner)
            out_ref[at, :bins, :] = real_sum[:, k * LANES : (k + 1) * LANES]
            out_ref[at, bins:, :] = imag_sum[:, k * LANES : (k + 1) * LANES]


def place_kernel(in_ref, out_ref):
    devices, rows, _ = in_ref.shape
    bins = rows // 2
    row = lax.broadcasted_iota(jnp.int32, (LANES, LANES), 0)
    lane = lax.broadcasted_iota(jnp.int32, (LANES, LANES), 1)
    order = (lane == CLASSES * (row % bins) + row // bins).astype(jnp.float32).astype(jnp.bfloat16)
    for kind in (0, 1):
        for j in range(devices // CLASSES):
            sources = range(j, devices, devices // CLASSES)
            places = [RESULT_RANKS.index(SPECTRA_RANKS[u]) for u in sources]
            block = jnp.concatenate([in_ref[at, kind * bins : (kind + 1) * bins, :] for at in places], axis=0).T
            natural = jnp.dot(block, order, preferred_element_type=jnp.float32)
            place = kind * BINS + j * LANES
            out_ref[:, place : place + LANES] = natural.astype(jnp.bfloat16)


def by_bins(records, first_station, second_region, second_station):
    regions, slabs = lax.axis_size("region"), lax.axis_size("slab")
    devices = regions * slabs
    stations, samples = records.shape
    parts = slabs // SEG
    rows = stations // parts
    count = rows // 2
    pair_count = first_station.shape[0]
    vmem = pl.BlockSpec(memory_space=pltpu.VMEM)
    limit = pltpu.CompilerParams(vmem_limit_bytes=12 << 20)
    divided = pl.pallas_call(
        divide_kernel,
        out_shape=[jax.ShapeDtypeStruct((rows, samples), records.dtype)] * parts,
        in_specs=[vmem],
        out_specs=[vmem] * parts,
        compiler_params=limit,
        name="divide",
    )(records)
    arrived = list(divided)
    for k in range(parts - 1, 0, -1):
        arrived[k] = lax.ppermute(divided[k], "slab", [(i, i ^ k) for i in range(slabs)])
    named = first_station + EXACT * second_station + EXACT * EXACT * second_region.reshape(-1)
    prepared = pl.pallas_call(
        prepare_kernel,
        out_shape=[
            jax.ShapeDtypeStruct((INDEX_ROWS, pair_count), jnp.bfloat16),
            jax.ShapeDtypeStruct((TAPER_ROWS, samples), jnp.float32),
            jax.ShapeDtypeStruct((CLASSES * samples, 2 * WIDTH), jnp.bfloat16),
        ],
        in_specs=[vmem] * 2,
        out_specs=[vmem] * 3,
        compiler_params=limit,
        cost_estimate=pl.CostEstimate(flops=NFFT * BINS, bytes_accessed=NFFT * BINS, transcendentals=0),
        name="prepare",
    )(named.reshape(1, -1), jnp.asarray(constant_rows()))
    sent = pl.pallas_call(
        spectra_kernel,
        out_shape=jax.ShapeDtypeStruct((devices * (count + INDEX_ROWS), LANES), jnp.bfloat16),
        in_specs=[vmem] * (parts + 3),
        out_specs=vmem,
        compiler_params=limit,
        name="spectra",
    )(*arrived, *prepared)
    blocks = sent.reshape(devices, (count + INDEX_ROWS) // INDEX_ROWS, INDEX_ROWS, LANES)
    table = lax.all_to_all(blocks, AXES, split_axis=0, concat_axis=0, tiled=True, axis_index_groups=[SPECTRA_RANKS]).reshape(sent.shape)
    partial = pl.pallas_call(
        functools.partial(cross_kernel, regions, slabs),
        out_shape=jax.ShapeDtypeStruct((devices, LANES // 2, pair_count), jnp.bfloat16),
        in_specs=[vmem],
        out_specs=vmem,
        scratch_shapes=[pltpu.VMEM((regions * LANES, stations), jnp.bfloat16)],
        compiler_params=limit,
        name="cross",
    )(table)
    pieces = lax.all_to_all(partial, AXES, split_axis=0, concat_axis=0, tiled=True, axis_index_groups=[RESULT_RANKS])
    return pl.pallas_call(
        place_kernel,
        out_shape=jax.ShapeDtypeStruct((pair_count, 2 * BINS), jnp.bfloat16),
        in_specs=[vmem],
        out_specs=vmem,
        compiler_params=limit,
        name="place",
    )(pieces)


def dft_table():
    sample = jnp.arange(NFFT, dtype=jnp.int32)[:, None]
    frequency = jnp.arange(BINS, dtype=jnp.int32)[None, :]
    phase = (sample * frequency % NFFT).astype(jnp.float32) * (2.0 * math.pi / NFFT)
    return jnp.concatenate([jnp.cos(phase), -jnp.sin(phase)], axis=1).astype(jnp.bfloat16)


def whitened(traces):
    count = traces.shape[0]
    signal = traces.astype(jnp.float32).reshape(count * SEG, NFFT)
    signal = signal - jnp.mean(signal, axis=1, keepdims=True)
    position = jnp.arange(NFFT, dtype=jnp.int32).astype(jnp.float32)
    taper = 0.5 - 0.5 * jnp.cos(position * (2.0 * math.pi / NFFT))
    tapered = (signal * taper[None, :]).astype(jnp.bfloat16)
    spectrum = jnp.dot(tapered, dft_table(), preferred_element_type=jnp.float32)
    real_part = spectrum[:, :BINS]
    imag_part = spectrum[:, BINS:]
    amplitude = jnp.sqrt(real_part * real_part + imag_part * imag_part + 1e-06)
    padded = jnp.pad(amplitude, ((0, 0), (HALF, HALF)))
    smooth = jnp.zeros_like(amplitude)
    for offset in range(2 * HALF + 1):
        smooth = smooth + padded[:, offset : offset + BINS]
    smooth = smooth / (2 * HALF + 1)
    level = jnp.mean(amplitude, axis=1, keepdims=True)
    divisor = smooth + level + 1e-06
    white = spectrum / jnp.concatenate([divisor, divisor], axis=1)
    return white.astype(jnp.bfloat16).reshape(count, SEG * NFFT)


def cross(first_rows, second_rows):
    left = first_rows.astype(jnp.float32).reshape(first_rows.shape[:-1] + (SEG, 2, BINS))
    right = second_rows.astype(jnp.float32).reshape(second_rows.shape[:-1] + (SEG, 2, BINS))
    real_sum = jnp.mean(left[..., 0, :] * right[..., 0, :] + left[..., 1, :] * right[..., 1, :], axis=-2)
    imag_sum = jnp.mean(left[..., 0, :] * right[..., 1, :] - left[..., 1, :] * right[..., 0, :], axis=-2)
    return jnp.concatenate([real_sum, imag_sum], axis=-1).astype(jnp.bfloat16)


def by_rows(records, first_station, second_region, second_station):
    regions = lax.axis_size("region")
    pair_count = first_station.shape[0]
    capacity = max(2, pair_count // regions + pair_count // 16)
    arrived = lax.all_to_all(records, "slab", split_axis=0, concat_axis=1, tiled=True)
    spectra = whitened(arrived)
    width = spectra.shape[1]
    target = second_region[:, 0]
    onehot = (target[:, None] == jnp.arange(regions, dtype=jnp.int32)[None, :]).astype(jnp.int32)
    ranking = jnp.sum((jnp.cumsum(onehot, axis=0) - onehot) * onehot, axis=1)
    slot_index = target * capacity + ranking
    requests = jnp.zeros((regions * capacity,), jnp.int32).at[slot_index].set(second_station).reshape(regions, capacity)
    incoming = lax.all_to_all(requests, "region", split_axis=0, concat_axis=0, tiled=True)
    wanted = jnp.concatenate([first_station, incoming.reshape(-1)])
    piece = lax.all_gather(spectra, "slab", axis=0, tiled=True)
    picked = jnp.take(piece, wanted, axis=0)
    first_rows = picked[:pair_count]
    served = picked[pair_count:]
    returned = lax.all_to_all(
        served.reshape(regions, capacity, width), "region", split_axis=0, concat_axis=0, tiled=True
    )
    second_rows = jnp.take(returned.reshape(regions * capacity, width), slot_index, axis=0)
    return cross(first_rows, second_rows)


def local(records, first_station, second_region, second_station):
    slabs = lax.axis_size("slab")
    devices = lax.axis_size("region") * slabs
    fits = (
        devices * LANES == 4 * BINS
        and devices == len(SPECTRA_RANKS)
        and records.shape == (EXACT, NFFT * SEG // slabs)
        and slabs == 4 * SEG
        and first_station.shape[0] == LANES
    )
    plan = by_bins if fits else by_rows
    return plan(records, first_station, second_region, second_station)


def solution(mesh):
    placed = (
        P(AXES[0], AXES[1]),
        P(AXES),
        P(AXES, None),
        P(AXES),
    )
    return jax.shard_map(local, mesh=mesh, in_specs=placed, out_specs=P(AXES, None), check_vma=False)
```

```python
import functools
import math

import jax
import jax.numpy as jnp
import numpy as np
from jax import lax
from jax.experimental import pallas as pl
from jax.experimental.pallas import tpu as pltpu
from jax.sharding import PartitionSpec as P

NFFT = 2048
BINS = 1024
SEG = 2
HALF = 4
LANES = 128
INDEX_ROWS = 4
CLASSES = 4
WIDTH = BINS // CLASSES
COARSE, FINE = 16, 32
TAPER_ROWS = 8
EXACT = 256
AXES = ("region", "slab")
SPECTRA_RANKS = [
    16, 8, 24, 0, 15, 23, 7, 31, 26, 10, 18, 2, 19, 11, 27, 3,
    20, 13, 28, 4, 21, 12, 29, 5, 22, 14, 30, 6, 17, 9, 25, 1,
]
RESULT_RANKS = [
    16, 0, 8, 24, 2, 18, 10, 26, 15, 23, 7, 31, 3, 11, 19, 27,
    4, 12, 25, 28, 17, 13, 21, 29, 6, 14, 22, 30, 1, 9, 5, 20,
]


def constant_rows():
    rows = []
    for pair in range(CLASSES // 2):
        frequency = np.concatenate([CLASSES * np.arange(WIDTH, dtype=np.int64) + 2 * pair + side for side in (0, 1)])
        for sample in (FINE * np.arange(COARSE, dtype=np.int64), np.arange(FINE, dtype=np.int64)):
            phase = (sample[:, None] * frequency[None, :] % NFFT) * (2.0 * math.pi / NFFT)
            rows += [np.cos(phase), np.sin(phase)]
    angle = np.arange(NFFT, dtype=np.float32) * np.float32(2.0 * math.pi / NFFT)
    cosine = np.cos(angle.astype(np.float64)).astype(np.float32)
    taper = (np.float32(0.5) - np.float32(0.5) * cosine).reshape(CLASSES, -1)
    rows.append(np.pad(taper, ((0, TAPER_ROWS - CLASSES), (0, 0))))
    return np.concatenate(rows, axis=0).astype(np.float32)


def prepare_kernel(named_ref, rows_ref, index_ref, taper_ref, table_ref):
    row = lax.broadcasted_iota(jnp.int32, index_ref.shape, 0)
    named = lax.rem(jnp.right_shift(named_ref[...], 8 * row), EXACT)
    index_ref[...] = named.astype(jnp.float32).astype(jnp.bfloat16)
    held = 2 * (COARSE + FINE)
    taper_ref[...] = rows_ref[held * CLASSES // 2 :, :]
    for pair in range(CLASSES // 2):
        at = pair * held
        fine_cos = rows_ref[at + 2 * COARSE : at + 2 * COARSE + FINE, :]
        fine_sin = rows_ref[at + 2 * COARSE + FINE : at + held, :]

        def block(i, _):
            coarse_cos = rows_ref[pl.ds(at + i, 1), :]
            coarse_sin = rows_ref[pl.ds(at + COARSE + i, 1), :]
            cosine = (coarse_cos * fine_cos - coarse_sin * fine_sin).astype(jnp.bfloat16)
            sine = (-coarse_sin * fine_cos - coarse_cos * fine_sin).astype(jnp.bfloat16)
            for side in (0, 1):
                first = (2 * pair + side) * FINE * COARSE + i * FINE
                place = pl.ds(pl.multiple_of(first, FINE), FINE)
                table_ref[place, :WIDTH] = cosine[:, side * WIDTH : (side + 1) * WIDTH]
                table_ref[place, WIDTH:] = sine[:, side * WIDTH : (side + 1) * WIDTH]
            return 0

        lax.fori_loop(0, COARSE, block, 0, unroll=4)


def divide_kernel(records_ref, *targets):
    parts = len(targets)
    rows = targets[0].shape[0]
    own = lax.rem(lax.axis_index("slab"), parts)
    for k, target in enumerate(targets):
        first = pl.multiple_of(jnp.bitwise_xor(own, k) * rows, rows)
        target[...] = records_ref[pl.ds(first, rows), :]


def shifted(values, step):
    width = values.shape[1]
    lane = lax.broadcasted_iota(jnp.int32, values.shape, 1)
    moved = pltpu.roll(values, (-step) % width, 1)
    return jnp.where((lane + step >= 0) & (lane + step < width), moved, 0.0)


def two_terms(values):
    coarse = values.astype(jnp.bfloat16)
    fine = (values - coarse.astype(jnp.float32)).astype(jnp.bfloat16)
    return jnp.concatenate([coarse, fine], axis=0)


def spectra_kernel(*refs):
    parts = len(refs) - 4
    index_ref, taper_ref, table_ref, out_ref = refs[parts:]
    rows, samples = refs[0].shape
    count = rows // 2
    own = lax.rem(lax.axis_index("slab"), parts)
    blocks = [ref[...] for ref in refs[:parts]]
    for bit in range(parts.bit_length() - 1):
        swapped = jnp.bitwise_and(jnp.right_shift(own, bit), 1) == 1
        blocks = [jnp.where(swapped, blocks[k ^ (1 << bit)], blocks[k]) for k in range(parts)]
    blocks = [block.astype(jnp.float32) for block in blocks]
    mean = jnp.sum((blocks[0] + blocks[1]) + (blocks[2] + blocks[3]), axis=1, keepdims=True) * (1.0 / NFFT)
    blocks = [((block - mean) * taper_ref[j : j + 1, :]).astype(jnp.bfloat16) for j, block in enumerate(blocks)]
    blocks = [block.astype(jnp.float32) for block in blocks]

    def transformed(values, r):
        table = table_ref[r * samples : (r + 1) * samples, :]
        both = jnp.dot(two_terms(values), table, preferred_element_type=jnp.float32)
        both = both[: values.shape[0]] + both[values.shape[0] :]
        return both[:, :WIDTH], both[:, WIDTH:]

    added, taken = ([blocks[j] + sign * blocks[j + 2] for j in (0, 1)] for sign in (1.0, -1.0))
    spectrum = [None] * CLASSES
    spectrum[0] = transformed(added[0] + added[1], 0)
    spectrum[2] = transformed(added[0] - added[1], 2)
    for r, sign in ((1, 1.0), (3, -1.0)):
        with_cos, with_sin = transformed(jnp.concatenate(taken, axis=0), r)
        spectrum[r] = (with_cos[:rows] + sign * with_sin[rows:], with_sin[:rows] - sign * with_cos[rows:])
    size = [jnp.sqrt(re * re + im * im + 1e-06) for re, im in spectrum]
    every = (size[0] + size[1]) + (size[2] + size[3])
    level = jnp.sum(every, axis=1, keepdims=True) * (1.0 / BINS) + 1e-06
    before, after = ([shifted(part, step) for part in size] for step in (-1, 1))
    group = LANES // 4
    lane_group = lax.broadcasted_iota(jnp.int32, (count, LANES), 1) // group
    for r in range(CLASSES):
        smooth = every
        for part in before[r:] + after[: r + 1]:
            smooth = smooth + part
        scale = 1.0 / (smooth * (1.0 / (2 * HALF + 1)) + level)
        white = [(part * scale).astype(jnp.bfloat16) for part in spectrum[r]]
        for s in range(WIDTH // LANES):
            sources = [
                part[side * count : (side + 1) * count, s * LANES : (s + 1) * LANES] for side in (0, 1) for part in white
            ]
            for q in range(4):
                block = None
                for place, source in enumerate(sources):
                    turn = (place - q) * group % LANES
                    moved = pltpu.roll(source, turn, 1) if turn else source
                    block = moved if block is None else jnp.where(lane_group == place, moved, block)
                at = (r * WIDTH // group + 4 * s + q) * (count + INDEX_ROWS)
                out_ref[at : at + count, :] = block
                out_ref[at + count : at + count + INDEX_ROWS, :] = index_ref[...]


def cross_kernel(regions, slabs, table_ref, out_ref, flipped_ref):
    devices = regions * slabs
    rows = table_ref.shape[0] // devices
    count = rows - INDEX_ROWS
    parts = slabs // SEG
    wide = parts * count
    stations = 2 * wide
    bins = LANES // 4
    per_step = 2
    for region in range(regions):
        for segment in range(SEG):
            sources = [SPECTRA_RANKS.index(region * slabs + segment * parts + part) * rows for part in range(parts)]
            block = jnp.concatenate([table_ref[at : at + count, :] for at in sources], axis=0).T
            at = region * LANES + segment * 2 * bins
            for half in (0, 1):
                flipped_ref[at : at + 2 * bins, half * wide : (half + 1) * wide] = block[half * 2 * bins : (half + 1) * 2 * bins]
    column = lax.broadcasted_iota(jnp.int32, (stations, per_step * LANES), 0)
    half, part = column // wide, column % wide // count
    station = (part * 2 + half) * count + column % count
    station = station.astype(jnp.float32).astype(jnp.bfloat16)
    one, zero = jnp.ones((), jnp.bfloat16), jnp.zeros((), jnp.bfloat16)
    for i in range(devices // per_step):
        home, first_slab = i % regions, i // regions * per_step
        owners = [home * slabs + first_slab + k for k in range(per_step)]
        places = [SPECTRA_RANKS.index(owner) * rows for owner in owners]
        named = [table_ref[at + count : at + rows, :] for at in places]
        named = jnp.concatenate(named, axis=1)
        first, second, target = named[0:1], named[1:2], named[2:3].astype(jnp.float32)
        own = flipped_ref[home * LANES : (home + 1) * LANES, :]
        a = jnp.dot(own, jnp.where(station == first, one, zero), preferred_element_type=jnp.float32)
        pick_second = jnp.where(station == second, one, zero)
        b = None
        for region in range(regions):
            rows_of = flipped_ref[region * LANES : (region + 1) * LANES, :]
            candidate = jnp.dot(rows_of, pick_second, preferred_element_type=jnp.float32)
            b = candidate if b is None else jnp.where(target == region, candidate, b)
        real_sum, imag_sum = 0.0, 0.0
        for segment in range(SEG):
            at = 2 * segment * bins
            ar, ai = a[at : at + bins], a[at + bins : at + 2 * bins]
            br, bi = b[at : at + bins], b[at + bins : at + 2 * bins]
            real_sum = real_sum + (ar * br + ai * bi)
            imag_sum = imag_sum + (ar * bi - ai * br)
        real_sum = (real_sum * (1.0 / SEG)).astype(jnp.bfloat16)
        imag_sum = (imag_sum * (1.0 / SEG)).astype(jnp.bfloat16)
        for k, owner in enumerate(owners):
            at = RESULT_RANKS.index(owner)
            out_ref[at, :bins, :] = real_sum[:, k * LANES : (k + 1) * LANES]
            out_ref[at, bins:, :] = imag_sum[:, k * LANES : (k + 1) * LANES]


def place_kernel(in_ref, out_ref):
    devices, rows, _ = in_ref.shape
    bins = rows // 2
    row = lax.broadcasted_iota(jnp.int32, (LANES, LANES), 0)
    lane = lax.broadcasted_iota(jnp.int32, (LANES, LANES), 1)
    order = (lane == CLASSES * (row % bins) + row // bins).astype(jnp.float32).astype(jnp.bfloat16)
    for kind in (0, 1):
        for j in range(devices // CLASSES):
            sources = range(j, devices, devices // CLASSES)
            places = [RESULT_RANKS.index(SPECTRA_RANKS[u]) for u in sources]
            block = jnp.concatenate([in_ref[at, kind * bins : (kind + 1) * bins, :] for at in places], axis=0).T
            natural = jnp.dot(block, order, preferred_element_type=jnp.float32)
            place = kind * BINS + j * LANES
            out_ref[:, place : place + LANES] = natural.astype(jnp.bfloat16)


def by_bins(records, first_station, second_region, second_station):
    regions, slabs = lax.axis_size("region"), lax.axis_size("slab")
    devices = regions * slabs
    stations, samples = records.shape
    parts = slabs // SEG
    rows = stations // parts
    count = rows // 2
    pair_count = first_station.shape[0]
    vmem = pl.BlockSpec(memory_space=pltpu.VMEM)
    limit = pltpu.CompilerParams(vmem_limit_bytes=12 << 20)
    divided = pl.pallas_call(
        divide_kernel,
        out_shape=[jax.ShapeDtypeStruct((rows, samples), records.dtype)] * parts,
        in_specs=[vmem],
        out_specs=[vmem] * parts,
        compiler_params=limit,
        name="divide",
    )(records)
    arrived = list(divided)
    for k in range(parts - 1, 0, -1):
        arrived[k] = lax.ppermute(divided[k], "slab", [(i, i ^ k) for i in range(slabs)])
    named = first_station + EXACT * second_station + EXACT * EXACT * second_region.reshape(-1)
    prepared = pl.pallas_call(
        prepare_kernel,
        out_shape=[
            jax.ShapeDtypeStruct((INDEX_ROWS, pair_count), jnp.bfloat16),
            jax.ShapeDtypeStruct((TAPER_ROWS, samples), jnp.float32),
            jax.ShapeDtypeStruct((CLASSES * samples, 2 * WIDTH), jnp.bfloat16),
        ],
        in_specs=[vmem] * 2,
        out_specs=[vmem] * 3,
        compiler_params=limit,
        cost_estimate=pl.CostEstimate(flops=NFFT * BINS, bytes_accessed=NFFT * BINS, transcendentals=0),
        name="prepare",
    )(named.reshape(1, -1), jnp.asarray(constant_rows()))
    sent = pl.pallas_call(
        spectra_kernel,
        out_shape=jax.ShapeDtypeStruct((devices * (count + INDEX_ROWS), LANES), jnp.bfloat16),
        in_specs=[vmem] * (parts + 3),
        out_specs=vmem,
        compiler_params=limit,
        name="spectra",
    )(*arrived, *prepared)
    blocks = sent.reshape(devices, (count + INDEX_ROWS) // INDEX_ROWS, INDEX_ROWS, LANES)
    table = lax.all_to_all(blocks, AXES, split_axis=0, concat_axis=0, tiled=True, axis_index_groups=[SPECTRA_RANKS]).reshape(sent.shape)
    partial = pl.pallas_call(
        functools.partial(cross_kernel, regions, slabs),
        out_shape=jax.ShapeDtypeStruct((devices, LANES // 2, pair_count), jnp.bfloat16),
        in_specs=[vmem],
        out_specs=vmem,
        scratch_shapes=[pltpu.VMEM((regions * LANES, stations), jnp.bfloat16)],
        compiler_params=limit,
        name="cross",
    )(table)
    pieces = lax.all_to_all(partial, AXES, split_axis=0, concat_axis=0, tiled=True, axis_index_groups=[RESULT_RANKS])
    return pl.pallas_call(
        place_kernel,
        out_shape=jax.ShapeDtypeStruct((pair_count, 2 * BINS), jnp.bfloat16),
        in_specs=[vmem],
        out_specs=vmem,
        compiler_params=limit,
        name="place",
    )(pieces)


def dft_table():
    sample = jnp.arange(NFFT, dtype=jnp.int32)[:, None]
    frequency = jnp.arange(BINS, dtype=jnp.int32)[None, :]
    phase = (sample * frequency % NFFT).astype(jnp.float32) * (2.0 * math.pi / NFFT)
    return jnp.concatenate([jnp.cos(phase), -jnp.sin(phase)], axis=1).astype(jnp.bfloat16)


def whitened(traces):
    count = traces.shape[0]
    signal = traces.astype(jnp.float32).reshape(count * SEG, NFFT)
    signal = signal - jnp.mean(signal, axis=1, keepdims=True)
    position = jnp.arange(NFFT, dtype=jnp.int32).astype(jnp.float32)
    taper = 0.5 - 0.5 * jnp.cos(position * (2.0 * math.pi / NFFT))
    tapered = (signal * taper[None, :]).astype(jnp.bfloat16)
    spectrum = jnp.dot(tapered, dft_table(), preferred_element_type=jnp.float32)
    real_part = spectrum[:, :BINS]
    imag_part = spectrum[:, BINS:]
    amplitude = jnp.sqrt(real_part * real_part + imag_part * imag_part + 1e-06)
    padded = jnp.pad(amplitude, ((0, 0), (HALF, HALF)))
    smooth = jnp.zeros_like(amplitude)
    for offset in range(2 * HALF + 1):
        smooth = smooth + padded[:, offset : offset + BINS]
    smooth = smooth / (2 * HALF + 1)
    level = jnp.mean(amplitude, axis=1, keepdims=True)
    divisor = smooth + level + 1e-06
    white = spectrum / jnp.concatenate([divisor, divisor], axis=1)
    return white.astype(jnp.bfloat16).reshape(count, SEG * NFFT)


def cross(first_rows, second_rows):
    left = first_rows.astype(jnp.float32).reshape(first_rows.shape[:-1] + (SEG, 2, BINS))
    right = second_rows.astype(jnp.float32).reshape(second_rows.shape[:-1] + (SEG, 2, BINS))
    real_sum = jnp.mean(left[..., 0, :] * right[..., 0, :] + left[..., 1, :] * right[..., 1, :], axis=-2)
    imag_sum = jnp.mean(left[..., 0, :] * right[..., 1, :] - left[..., 1, :] * right[..., 0, :], axis=-2)
    return jnp.concatenate([real_sum, imag_sum], axis=-1).astype(jnp.bfloat16)


def by_rows(records, first_station, second_region, second_station):
    regions = lax.axis_size("region")
    pair_count = first_station.shape[0]
    capacity = max(2, pair_count // regions + pair_count // 16)
    arrived = lax.all_to_all(records, "slab", split_axis=0, concat_axis=1, tiled=True)
    spectra = whitened(arrived)
    width = spectra.shape[1]
    target = second_region[:, 0]
    onehot = (target[:, None] == jnp.arange(regions, dtype=jnp.int32)[None, :]).astype(jnp.int32)
    ranking = jnp.sum((jnp.cumsum(onehot, axis=0) - onehot) * onehot, axis=1)
    slot_index = target * capacity + ranking
    requests = jnp.zeros((regions * capacity,), jnp.int32).at[slot_index].set(second_station).reshape(regions, capacity)
    incoming = lax.all_to_all(requests, "region", split_axis=0, concat_axis=0, tiled=True)
    wanted = jnp.concatenate([first_station, incoming.reshape(-1)])
    piece = lax.all_gather(spectra, "slab", axis=0, tiled=True)
    picked = jnp.take(piece, wanted, axis=0)
    first_rows = picked[:pair_count]
    served = picked[pair_count:]
    returned = lax.all_to_all(
        served.reshape(regions, capacity, width), "region", split_axis=0, concat_axis=0, tiled=True
    )
    second_rows = jnp.take(returned.reshape(regions * capacity, width), slot_index, axis=0)
    return cross(first_rows, second_rows)


def local(records, first_station, second_region, second_station):
    slabs = lax.axis_size("slab")
    devices = lax.axis_size("region") * slabs
    fits = (
        devices * LANES == 4 * BINS
        and devices == len(SPECTRA_RANKS)
        and records.shape == (EXACT, NFFT * SEG // slabs)
        and slabs == 4 * SEG
        and first_station.shape[0] == LANES
    )
    plan = by_bins if fits else by_rows
    return plan(records, first_station, second_region, second_station)


def solution(mesh):
    placed = (
        P(AXES[0], AXES[1]),
        P(AXES),
        P(AXES, None),
        P(AXES),
    )
    return jax.shard_map(local, mesh=mesh, in_specs=placed, out_specs=P(AXES, None), check_vma=False)
```

```python
import functools
import math

import jax
import jax.numpy as jnp
import numpy as np
from jax import lax
from jax.experimental import pallas as pl
from jax.experimental.pallas import tpu as pltpu
from jax.sharding import PartitionSpec as P

NFFT = 2048
BINS = 1024
SEG = 2
HALF = 4
LANES = 128
INDEX_ROWS = 4
CLASSES = 4
WIDTH = BINS // CLASSES
COARSE, FINE = 16, 32
TAPER_ROWS = 8
EXACT = 256
AXES = ("region", "slab")
SPECTRA_RANKS = [
    24, 16, 8, 0, 15, 23, 7, 31, 26, 10, 18, 2, 19, 3, 11, 27,
    20, 13, 28, 4, 17, 9, 25, 1, 22, 14, 30, 6, 21, 12, 29, 5,
]
RESULT_RANKS = [
    16, 0, 8, 24, 17, 13, 21, 29, 15, 23, 7, 31, 3, 11, 19, 27,
    1, 9, 5, 20, 2, 18, 10, 26, 6, 14, 22, 30, 4, 12, 25, 28,
]


def constant_rows():
    rows = []
    for pair in range(CLASSES // 2):
        frequency = np.concatenate([CLASSES * np.arange(WIDTH, dtype=np.int64) + 2 * pair + side for side in (0, 1)])
        for sample in (FINE * np.arange(COARSE, dtype=np.int64), np.arange(FINE, dtype=np.int64)):
            phase = (sample[:, None] * frequency[None, :] % NFFT) * (2.0 * math.pi / NFFT)
            rows += [np.cos(phase), np.sin(phase)]
    angle = np.arange(NFFT, dtype=np.float32) * np.float32(2.0 * math.pi / NFFT)
    cosine = np.cos(angle.astype(np.float64)).astype(np.float32)
    taper = (np.float32(0.5) - np.float32(0.5) * cosine).reshape(CLASSES, -1)
    rows.append(np.pad(taper, ((0, TAPER_ROWS - CLASSES), (0, 0))))
    return np.concatenate(rows, axis=0).astype(np.float32)


def prepare_kernel(named_ref, rows_ref, index_ref, taper_ref, table_ref):
    row = lax.broadcasted_iota(jnp.int32, index_ref.shape, 0)
    named = lax.rem(jnp.right_shift(named_ref[...], 8 * row), EXACT)
    index_ref[...] = named.astype(jnp.float32).astype(jnp.bfloat16)
    held = 2 * (COARSE + FINE)
    taper_ref[...] = rows_ref[held * CLASSES // 2 :, :]
    for pair in range(CLASSES // 2):
        at = pair * held
        fine_cos = rows_ref[at + 2 * COARSE : at + 2 * COARSE + FINE, :]
        fine_sin = rows_ref[at + 2 * COARSE + FINE : at + held, :]

        def block(i, _):
            coarse_cos = rows_ref[pl.ds(at + i, 1), :]
            coarse_sin = rows_ref[pl.ds(at + COARSE + i, 1), :]
            cosine = (coarse_cos * fine_cos - coarse_sin * fine_sin).astype(jnp.bfloat16)
            sine = (-coarse_sin * fine_cos - coarse_cos * fine_sin).astype(jnp.bfloat16)
            for side in (0, 1):
                first = (2 * pair + side) * FINE * COARSE + i * FINE
                place = pl.ds(pl.multiple_of(first, FINE), FINE)
                table_ref[place, :WIDTH] = cosine[:, side * WIDTH : (side + 1) * WIDTH]
                table_ref[place, WIDTH:] = sine[:, side * WIDTH : (side + 1) * WIDTH]
            return 0

        lax.fori_loop(0, COARSE, block, 0, unroll=4)


def divide_kernel(records_ref, *targets):
    parts = len(targets)
    rows = targets[0].shape[0]
    own = lax.rem(lax.axis_index("slab"), parts)
    for k, target in enumerate(targets):
        first = pl.multiple_of(jnp.bitwise_xor(own, k) * rows, rows)
        target[...] = records_ref[pl.ds(first, rows), :]


def shifted(values, step):
    width = values.shape[1]
    lane = lax.broadcasted_iota(jnp.int32, values.shape, 1)
    moved = pltpu.roll(values, (-step) % width, 1)
    return jnp.where((lane + step >= 0) & (lane + step < width), moved, 0.0)


def two_terms(values):
    coarse = values.astype(jnp.bfloat16)
    fine = (values - coarse.astype(jnp.float32)).astype(jnp.bfloat16)
    return jnp.concatenate([coarse, fine], axis=0)


def spectra_kernel(*refs):
    parts = len(refs) - 4
    index_ref, taper_ref, table_ref, out_ref = refs[parts:]
    rows, samples = refs[0].shape
    count = rows // 2
    own = lax.rem(lax.axis_index("slab"), parts)
    blocks = [ref[...] for ref in refs[:parts]]
    for bit in range(parts.bit_length() - 1):
        swapped = jnp.bitwise_and(jnp.right_shift(own, bit), 1) == 1
        blocks = [jnp.where(swapped, blocks[k ^ (1 << bit)], blocks[k]) for k in range(parts)]
    blocks = [block.astype(jnp.float32) for block in blocks]
    mean = jnp.sum((blocks[0] + blocks[1]) + (blocks[2] + blocks[3]), axis=1, keepdims=True) * (1.0 / NFFT)
    blocks = [((block - mean) * taper_ref[j : j + 1, :]).astype(jnp.bfloat16) for j, block in enumerate(blocks)]
    blocks = [block.astype(jnp.float32) for block in blocks]

    def transformed(values, r):
        table = table_ref[r * samples : (r + 1) * samples, :]
        both = jnp.dot(two_terms(values), table, preferred_element_type=jnp.float32)
        both = both[: values.shape[0]] + both[values.shape[0] :]
        return both[:, :WIDTH], both[:, WIDTH:]

    added, taken = ([blocks[j] + sign * blocks[j + 2] for j in (0, 1)] for sign in (1.0, -1.0))
    spectrum = [None] * CLASSES
    spectrum[0] = transformed(added[0] + added[1], 0)
    spectrum[2] = transformed(added[0] - added[1], 2)
    for r, sign in ((1, 1.0), (3, -1.0)):
        with_cos, with_sin = transformed(jnp.concatenate(taken, axis=0), r)
        spectrum[r] = (with_cos[:rows] + sign * with_sin[rows:], with_sin[:rows] - sign * with_cos[rows:])
    size = [jnp.sqrt(re * re + im * im + 1e-06) for re, im in spectrum]
    every = (size[0] + size[1]) + (size[2] + size[3])
    level = jnp.sum(every, axis=1, keepdims=True) * (1.0 / BINS) + 1e-06
    before, after = ([shifted(part, step) for part in size] for step in (-1, 1))
    group = LANES // 4
    lane_group = lax.broadcasted_iota(jnp.int32, (count, LANES), 1) // group
    for r in range(CLASSES):
        smooth = every
        for part in before[r:] + after[: r + 1]:
            smooth = smooth + part
        scale = 1.0 / (smooth * (1.0 / (2 * HALF + 1)) + level)
        white = [(part * scale).astype(jnp.bfloat16) for part in spectrum[r]]
        for s in range(WIDTH // LANES):
            sources = [
                part[side * count : (side + 1) * count, s * LANES : (s + 1) * LANES] for side in (0, 1) for part in white
            ]
            for q in range(4):
                block = None
                for place, source in enumerate(sources):
                    turn = (place - q) * group % LANES
                    moved = pltpu.roll(source, turn, 1) if turn else source
                    block = moved if block is None else jnp.where(lane_group == place, moved, block)
                at = (r * WIDTH // group + 4 * s + q) * (count + INDEX_ROWS)
                out_ref[at : at + count, :] = block
                out_ref[at + count : at + count + INDEX_ROWS, :] = index_ref[...]


def cross_kernel(regions, slabs, table_ref, out_ref, flipped_ref):
    devices = regions * slabs
    rows = table_ref.shape[0] // devices
    count = rows - INDEX_ROWS
    parts = slabs // SEG
    wide = parts * count
    stations = 2 * wide
    bins = LANES // 4
    per_step = 2
    for region in range(regions):
        for segment in range(SEG):
            sources = [SPECTRA_RANKS.index(region * slabs + segment * parts + part) * rows for part in range(parts)]
            block = jnp.concatenate([table_ref[at : at + count, :] for at in sources], axis=0).T
            at = region * LANES + segment * 2 * bins
            for half in (0, 1):
                flipped_ref[at : at + 2 * bins, half * wide : (half + 1) * wide] = block[half * 2 * bins : (half + 1) * 2 * bins]
    column = lax.broadcasted_iota(jnp.int32, (stations, per_step * LANES), 0)
    half, part = column // wide, column % wide // count
    station = (part * 2 + half) * count + column % count
    station = station.astype(jnp.float32).astype(jnp.bfloat16)
    one, zero = jnp.ones((), jnp.bfloat16), jnp.zeros((), jnp.bfloat16)
    for i in range(devices // per_step):
        home, first_slab = i % regions, i // regions * per_step
        owners = [home * slabs + first_slab + k for k in range(per_step)]
        places = [SPECTRA_RANKS.index(owner) * rows for owner in owners]
        named = [table_ref[at + count : at + rows, :] for at in places]
        named = jnp.concatenate(named, axis=1)
        first, second, target = named[0:1], named[1:2], named[2:3].astype(jnp.float32)
        own = flipped_ref[home * LANES : (home + 1) * LANES, :]
        a = jnp.dot(own, jnp.where(station == first, one, zero), preferred_element_type=jnp.float32)
        pick_second = jnp.where(station == second, one, zero)
        b = None
        for region in range(regions):
            rows_of = flipped_ref[region * LANES : (region + 1) * LANES, :]
            candidate = jnp.dot(rows_of, pick_second, preferred_element_type=jnp.float32)
            b = candidate if b is None else jnp.where(target == region, candidate, b)
        real_sum, imag_sum = 0.0, 0.0
        for segment in range(SEG):
            at = 2 * segment * bins
            ar, ai = a[at : at + bins], a[at + bins : at + 2 * bins]
            br, bi = b[at : at + bins], b[at + bins : at + 2 * bins]
            real_sum = real_sum + (ar * br + ai * bi)
            imag_sum = imag_sum + (ar * bi - ai * br)
        real_sum = (real_sum * (1.0 / SEG)).astype(jnp.bfloat16)
        imag_sum = (imag_sum * (1.0 / SEG)).astype(jnp.bfloat16)
        for k, owner in enumerate(owners):
            at = RESULT_RANKS.index(owner)
            out_ref[at, :bins, :] = real_sum[:, k * LANES : (k + 1) * LANES]
            out_ref[at, bins:, :] = imag_sum[:, k * LANES : (k + 1) * LANES]


def place_kernel(in_ref, out_ref):
    devices, rows, _ = in_ref.shape
    bins = rows // 2
    row = lax.broadcasted_iota(jnp.int32, (LANES, LANES), 0)
    lane = lax.broadcasted_iota(jnp.int32, (LANES, LANES), 1)
    order = (lane == CLASSES * (row % bins) + row // bins).astype(jnp.float32).astype(jnp.bfloat16)
    for kind in (0, 1):
        for j in range(devices // CLASSES):
            sources = range(j, devices, devices // CLASSES)
            places = [RESULT_RANKS.index(SPECTRA_RANKS[u]) for u in sources]
            block = jnp.concatenate([in_ref[at, kind * bins : (kind + 1) * bins, :] for at in places], axis=0).T
            natural = jnp.dot(block, order, preferred_element_type=jnp.float32)
            place = kind * BINS + j * LANES
            out_ref[:, place : place + LANES] = natural.astype(jnp.bfloat16)


def by_bins(records, first_station, second_region, second_station):
    regions, slabs = lax.axis_size("region"), lax.axis_size("slab")
    devices = regions * slabs
    stations, samples = records.shape
    parts = slabs // SEG
    rows = stations // parts
    count = rows // 2
    pair_count = first_station.shape[0]
    vmem = pl.BlockSpec(memory_space=pltpu.VMEM)
    limit = pltpu.CompilerParams(vmem_limit_bytes=12 << 20)
    divided = pl.pallas_call(
        divide_kernel,
        out_shape=[jax.ShapeDtypeStruct((rows, samples), records.dtype)] * parts,
        in_specs=[vmem],
        out_specs=[vmem] * parts,
        compiler_params=limit,
        name="divide",
    )(records)
    arrived = list(divided)
    for k in range(parts - 1, 0, -1):
        arrived[k] = lax.ppermute(divided[k], "slab", [(i, i ^ k) for i in range(slabs)])
    named = first_station + EXACT * second_station + EXACT * EXACT * second_region.reshape(-1)
    prepared = pl.pallas_call(
        prepare_kernel,
        out_shape=[
            jax.ShapeDtypeStruct((INDEX_ROWS, pair_count), jnp.bfloat16),
            jax.ShapeDtypeStruct((TAPER_ROWS, samples), jnp.float32),
            jax.ShapeDtypeStruct((CLASSES * samples, 2 * WIDTH), jnp.bfloat16),
        ],
        in_specs=[vmem] * 2,
        out_specs=[vmem] * 3,
        compiler_params=limit,
        cost_estimate=pl.CostEstimate(flops=NFFT * BINS, bytes_accessed=NFFT * BINS, transcendentals=0),
        name="prepare",
    )(named.reshape(1, -1), jnp.asarray(constant_rows()))
    sent = pl.pallas_call(
        spectra_kernel,
        out_shape=jax.ShapeDtypeStruct((devices * (count + INDEX_ROWS), LANES), jnp.bfloat16),
        in_specs=[vmem] * (parts + 3),
        out_specs=vmem,
        compiler_params=limit,
        name="spectra",
    )(*arrived, *prepared)
    blocks = sent.reshape(devices, (count + INDEX_ROWS) // INDEX_ROWS, INDEX_ROWS, LANES)
    table = lax.all_to_all(blocks, AXES, split_axis=0, concat_axis=0, tiled=True, axis_index_groups=[SPECTRA_RANKS]).reshape(sent.shape)
    partial = pl.pallas_call(
        functools.partial(cross_kernel, regions, slabs),
        out_shape=jax.ShapeDtypeStruct((devices, LANES // 2, pair_count), jnp.bfloat16),
        in_specs=[vmem],
        out_specs=vmem,
        scratch_shapes=[pltpu.VMEM((regions * LANES, stations), jnp.bfloat16)],
        compiler_params=limit,
        name="cross",
    )(table)
    pieces = lax.all_to_all(partial, AXES, split_axis=0, concat_axis=0, tiled=True, axis_index_groups=[RESULT_RANKS])
    return pl.pallas_call(
        place_kernel,
        out_shape=jax.ShapeDtypeStruct((pair_count, 2 * BINS), jnp.bfloat16),
        in_specs=[vmem],
        out_specs=vmem,
        compiler_params=limit,
        name="place",
    )(pieces)


def dft_table():
    sample = jnp.arange(NFFT, dtype=jnp.int32)[:, None]
    frequency = jnp.arange(BINS, dtype=jnp.int32)[None, :]
    phase = (sample * frequency % NFFT).astype(jnp.float32) * (2.0 * math.pi / NFFT)
    return jnp.concatenate([jnp.cos(phase), -jnp.sin(phase)], axis=1).astype(jnp.bfloat16)


def whitened(traces):
    count = traces.shape[0]
    signal = traces.astype(jnp.float32).reshape(count * SEG, NFFT)
    signal = signal - jnp.mean(signal, axis=1, keepdims=True)
    position = jnp.arange(NFFT, dtype=jnp.int32).astype(jnp.float32)
    taper = 0.5 - 0.5 * jnp.cos(position * (2.0 * math.pi / NFFT))
    tapered = (signal * taper[None, :]).astype(jnp.bfloat16)
    spectrum = jnp.dot(tapered, dft_table(), preferred_element_type=jnp.float32)
    real_part = spectrum[:, :BINS]
    imag_part = spectrum[:, BINS:]
    amplitude = jnp.sqrt(real_part * real_part + imag_part * imag_part + 1e-06)
    padded = jnp.pad(amplitude, ((0, 0), (HALF, HALF)))
    smooth = jnp.zeros_like(amplitude)
    for offset in range(2 * HALF + 1):
        smooth = smooth + padded[:, offset : offset + BINS]
    smooth = smooth / (2 * HALF + 1)
    level = jnp.mean(amplitude, axis=1, keepdims=True)
    divisor = smooth + level + 1e-06
    white = spectrum / jnp.concatenate([divisor, divisor], axis=1)
    return white.astype(jnp.bfloat16).reshape(count, SEG * NFFT)


def cross(first_rows, second_rows):
    left = first_rows.astype(jnp.float32).reshape(first_rows.shape[:-1] + (SEG, 2, BINS))
    right = second_rows.astype(jnp.float32).reshape(second_rows.shape[:-1] + (SEG, 2, BINS))
    real_sum = jnp.mean(left[..., 0, :] * right[..., 0, :] + left[..., 1, :] * right[..., 1, :], axis=-2)
    imag_sum = jnp.mean(left[..., 0, :] * right[..., 1, :] - left[..., 1, :] * right[..., 0, :], axis=-2)
    return jnp.concatenate([real_sum, imag_sum], axis=-1).astype(jnp.bfloat16)


def by_rows(records, first_station, second_region, second_station):
    regions = lax.axis_size("region")
    pair_count = first_station.shape[0]
    capacity = max(2, pair_count // regions + pair_count // 16)
    arrived = lax.all_to_all(records, "slab", split_axis=0, concat_axis=1, tiled=True)
    spectra = whitened(arrived)
    width = spectra.shape[1]
    target = second_region[:, 0]
    onehot = (target[:, None] == jnp.arange(regions, dtype=jnp.int32)[None, :]).astype(jnp.int32)
    ranking = jnp.sum((jnp.cumsum(onehot, axis=0) - onehot) * onehot, axis=1)
    slot_index = target * capacity + ranking
    requests = jnp.zeros((regions * capacity,), jnp.int32).at[slot_index].set(second_station).reshape(regions, capacity)
    incoming = lax.all_to_all(requests, "region", split_axis=0, concat_axis=0, tiled=True)
    wanted = jnp.concatenate([first_station, incoming.reshape(-1)])
    piece = lax.all_gather(spectra, "slab", axis=0, tiled=True)
    picked = jnp.take(piece, wanted, axis=0)
    first_rows = picked[:pair_count]
    served = picked[pair_count:]
    returned = lax.all_to_all(
        served.reshape(regions, capacity, width), "region", split_axis=0, concat_axis=0, tiled=True
    )
    second_rows = jnp.take(returned.reshape(regions * capacity, width), slot_index, axis=0)
    return cross(first_rows, second_rows)


def local(records, first_station, second_region, second_station):
    slabs = lax.axis_size("slab")
    devices = lax.axis_size("region") * slabs
    fits = (
        devices * LANES == 4 * BINS
        and devices == len(SPECTRA_RANKS)
        and records.shape == (EXACT, NFFT * SEG // slabs)
        and slabs == 4 * SEG
        and first_station.shape[0] == LANES
    )
    plan = by_bins if fits else by_rows
    return plan(records, first_station, second_region, second_station)


def solution(mesh):
    placed = (
        P(AXES[0], AXES[1]),
        P(AXES),
        P(AXES, None),
        P(AXES),
    )
    return jax.shard_map(local, mesh=mesh, in_specs=placed, out_specs=P(AXES, None), check_vma=False)
```

```python
import functools
import math

import jax
import jax.numpy as jnp
import numpy as np
from jax import lax
from jax.experimental import pallas as pl
from jax.experimental.pallas import tpu as pltpu
from jax.sharding import PartitionSpec as P

NFFT = 2048
BINS = 1024
SEG = 2
HALF = 4
LANES = 128
INDEX_ROWS = 4
CLASSES = 4
WIDTH = BINS // CLASSES
COARSE, FINE = 16, 32
TAPER_ROWS = 8
EXACT = 256
AXES = ("region", "slab")
SPECTRA_RANKS = [
    24, 16, 8, 0, 15, 23, 7, 31, 26, 10, 18, 2, 19, 3, 11, 27,
    20, 13, 28, 4, 17, 9, 25, 1, 22, 14, 30, 6, 21, 12, 29, 5,
]
RESULT_RANKS = [
    16, 0, 8, 24, 2, 18, 10, 26, 15, 23, 7, 31, 3, 11, 19, 27,
    4, 12, 25, 28, 17, 13, 21, 29, 6, 14, 22, 30, 1, 9, 5, 20,
]


def constant_rows():
    rows = []
    for pair in range(CLASSES // 2):
        frequency = np.concatenate([CLASSES * np.arange(WIDTH, dtype=np.int64) + 2 * pair + side for side in (0, 1)])
        for sample in (FINE * np.arange(COARSE, dtype=np.int64), np.arange(FINE, dtype=np.int64)):
            phase = (sample[:, None] * frequency[None, :] % NFFT) * (2.0 * math.pi / NFFT)
            rows += [np.cos(phase), np.sin(phase)]
    angle = np.arange(NFFT, dtype=np.float32) * np.float32(2.0 * math.pi / NFFT)
    cosine = np.cos(angle.astype(np.float64)).astype(np.float32)
    taper = (np.float32(0.5) - np.float32(0.5) * cosine).reshape(CLASSES, -1)
    rows.append(np.pad(taper, ((0, TAPER_ROWS - CLASSES), (0, 0))))
    return np.concatenate(rows, axis=0).astype(np.float32)


def prepare_kernel(named_ref, rows_ref, index_ref, taper_ref, table_ref):
    row = lax.broadcasted_iota(jnp.int32, index_ref.shape, 0)
    named = lax.rem(jnp.right_shift(named_ref[...], 8 * row), EXACT)
    index_ref[...] = named.astype(jnp.float32).astype(jnp.bfloat16)
    held = 2 * (COARSE + FINE)
    taper_ref[...] = rows_ref[held * CLASSES // 2 :, :]
    for pair in range(CLASSES // 2):
        at = pair * held
        fine_cos = rows_ref[at + 2 * COARSE : at + 2 * COARSE + FINE, :]
        fine_sin = rows_ref[at + 2 * COARSE + FINE : at + held, :]

        def block(i, _):
            coarse_cos = rows_ref[pl.ds(at + i, 1), :]
            coarse_sin = rows_ref[pl.ds(at + COARSE + i, 1), :]
            cosine = (coarse_cos * fine_cos - coarse_sin * fine_sin).astype(jnp.bfloat16)
            sine = (-coarse_sin * fine_cos - coarse_cos * fine_sin).astype(jnp.bfloat16)
            for side in (0, 1):
                first = (2 * pair + side) * FINE * COARSE + i * FINE
                place = pl.ds(pl.multiple_of(first, FINE), FINE)
                table_ref[place, :WIDTH] = cosine[:, side * WIDTH : (side + 1) * WIDTH]
                table_ref[place, WIDTH:] = sine[:, side * WIDTH : (side + 1) * WIDTH]
            return 0

        lax.fori_loop(0, COARSE, block, 0, unroll=4)


def divide_kernel(records_ref, *targets):
    parts = len(targets)
    rows = targets[0].shape[0]
    own = lax.rem(lax.axis_index("slab"), parts)
    for k, target in enumerate(targets):
        first = pl.multiple_of(jnp.bitwise_xor(own, k) * rows, rows)
        target[...] = records_ref[pl.ds(first, rows), :]


def shifted(values, step):
    width = values.shape[1]
    lane = lax.broadcasted_iota(jnp.int32, values.shape, 1)
    moved = pltpu.roll(values, (-step) % width, 1)
    return jnp.where((lane + step >= 0) & (lane + step < width), moved, 0.0)


def two_terms(values):
    coarse = values.astype(jnp.bfloat16)
    fine = (values - coarse.astype(jnp.float32)).astype(jnp.bfloat16)
    return jnp.concatenate([coarse, fine], axis=0)


def spectra_kernel(*refs):
    parts = len(refs) - 4
    index_ref, taper_ref, table_ref, out_ref = refs[parts:]
    rows, samples = refs[0].shape
    count = rows // 2
    own = lax.rem(lax.axis_index("slab"), parts)
    blocks = [ref[...] for ref in refs[:parts]]
    for bit in range(parts.bit_length() - 1):
        swapped = jnp.bitwise_and(jnp.right_shift(own, bit), 1) == 1
        blocks = [jnp.where(swapped, blocks[k ^ (1 << bit)], blocks[k]) for k in range(parts)]
    blocks = [block.astype(jnp.float32) for block in blocks]
    mean = jnp.sum((blocks[0] + blocks[1]) + (blocks[2] + blocks[3]), axis=1, keepdims=True) * (1.0 / NFFT)
    blocks = [((block - mean) * taper_ref[j : j + 1, :]).astype(jnp.bfloat16) for j, block in enumerate(blocks)]
    blocks = [block.astype(jnp.float32) for block in blocks]

    def transformed(values, r):
        table = table_ref[r * samples : (r + 1) * samples, :]
        both = jnp.dot(two_terms(values), table, preferred_element_type=jnp.float32)
        both = both[: values.shape[0]] + both[values.shape[0] :]
        return both[:, :WIDTH], both[:, WIDTH:]

    added, taken = ([blocks[j] + sign * blocks[j + 2] for j in (0, 1)] for sign in (1.0, -1.0))
    spectrum = [None] * CLASSES
    spectrum[0] = transformed(added[0] + added[1], 0)
    spectrum[2] = transformed(added[0] - added[1], 2)
    for r, sign in ((1, 1.0), (3, -1.0)):
        with_cos, with_sin = transformed(jnp.concatenate(taken, axis=0), r)
        spectrum[r] = (with_cos[:rows] + sign * with_sin[rows:], with_sin[:rows] - sign * with_cos[rows:])
    size = [jnp.sqrt(re * re + im * im + 1e-06) for re, im in spectrum]
    every = (size[0] + size[1]) + (size[2] + size[3])
    level = jnp.sum(every, axis=1, keepdims=True) * (1.0 / BINS) + 1e-06
    before, after = ([shifted(part, step) for part in size] for step in (-1, 1))
    group = LANES // 4
    lane_group = lax.broadcasted_iota(jnp.int32, (count, LANES), 1) // group
    for r in range(CLASSES):
        smooth = every
        for part in before[r:] + after[: r + 1]:
            smooth = smooth + part
        scale = 1.0 / (smooth * (1.0 / (2 * HALF + 1)) + level)
        white = [(part * scale).astype(jnp.bfloat16) for part in spectrum[r]]
        for s in range(WIDTH // LANES):
            sources = [
                part[side * count : (side + 1) * count, s * LANES : (s + 1) * LANES] for side in (0, 1) for part in white
            ]
            for q in range(4):
                block = None
                for place, source in enumerate(sources):
                    turn = (place - q) * group % LANES
                    moved = pltpu.roll(source, turn, 1) if turn else source
                    block = moved if block is None else jnp.where(lane_group == place, moved, block)
                at = (r * WIDTH // group + 4 * s + q) * (count + INDEX_ROWS)
                out_ref[at : at + count, :] = block
                out_ref[at + count : at + count + INDEX_ROWS, :] = index_ref[...]


def cross_kernel(regions, slabs, table_ref, out_ref, flipped_ref):
    devices = regions * slabs
    rows = table_ref.shape[0] // devices
    count = rows - INDEX_ROWS
    parts = slabs // SEG
    wide = parts * count
    stations = 2 * wide
    bins = LANES // 4
    per_step = 2
    for region in range(regions):
        for segment in range(SEG):
            sources = [SPECTRA_RANKS.index(region * slabs + segment * parts + part) * rows for part in range(parts)]
            block = jnp.concatenate([table_ref[at : at + count, :] for at in sources], axis=0).T
            at = region * LANES + segment * 2 * bins
            for half in (0, 1):
                flipped_ref[at : at + 2 * bins, half * wide : (half + 1) * wide] = block[half * 2 * bins : (half + 1) * 2 * bins]
    column = lax.broadcasted_iota(jnp.int32, (stations, per_step * LANES), 0)
    half, part = column // wide, column % wide // count
    station = (part * 2 + half) * count + column % count
    station = station.astype(jnp.float32).astype(jnp.bfloat16)
    one, zero = jnp.ones((), jnp.bfloat16), jnp.zeros((), jnp.bfloat16)
    for i in range(devices // per_step):
        home, first_slab = i % regions, i // regions * per_step
        owners = [home * slabs + first_slab + k for k in range(per_step)]
        places = [SPECTRA_RANKS.index(owner) * rows for owner in owners]
        named = [table_ref[at + count : at + rows, :] for at in places]
        named = jnp.concatenate(named, axis=1)
        first, second, target = named[0:1], named[1:2], named[2:3].astype(jnp.float32)
        own = flipped_ref[home * LANES : (home + 1) * LANES, :]
        a = jnp.dot(own, jnp.where(station == first, one, zero), preferred_element_type=jnp.float32)
        pick_second = jnp.where(station == second, one, zero)
        b = None
        for region in range(regions):
            rows_of = flipped_ref[region * LANES : (region + 1) * LANES, :]
            candidate = jnp.dot(rows_of, pick_second, preferred_element_type=jnp.float32)
            b = candidate if b is None else jnp.where(target == region, candidate, b)
        real_sum, imag_sum = 0.0, 0.0
        for segment in range(SEG):
            at = 2 * segment * bins
            ar, ai = a[at : at + bins], a[at + bins : at + 2 * bins]
            br, bi = b[at : at + bins], b[at + bins : at + 2 * bins]
            real_sum = real_sum + (ar * br + ai * bi)
            imag_sum = imag_sum + (ar * bi - ai * br)
        real_sum = (real_sum * (1.0 / SEG)).astype(jnp.bfloat16)
        imag_sum = (imag_sum * (1.0 / SEG)).astype(jnp.bfloat16)
        for k, owner in enumerate(owners):
            at = RESULT_RANKS.index(owner)
            out_ref[at, :bins, :] = real_sum[:, k * LANES : (k + 1) * LANES]
            out_ref[at, bins:, :] = imag_sum[:, k * LANES : (k + 1) * LANES]


def place_kernel(in_ref, out_ref):
    devices, rows, _ = in_ref.shape
    bins = rows // 2
    row = lax.broadcasted_iota(jnp.int32, (LANES, LANES), 0)
    lane = lax.broadcasted_iota(jnp.int32, (LANES, LANES), 1)
    order = (lane == CLASSES * (row % bins) + row // bins).astype(jnp.float32).astype(jnp.bfloat16)
    for kind in (0, 1):
        for j in range(devices // CLASSES):
            sources = range(j, devices, devices // CLASSES)
            places = [RESULT_RANKS.index(SPECTRA_RANKS[u]) for u in sources]
            block = jnp.concatenate([in_ref[at, kind * bins : (kind + 1) * bins, :] for at in places], axis=0).T
            natural = jnp.dot(block, order, preferred_element_type=jnp.float32)
            place = kind * BINS + j * LANES
            out_ref[:, place : place + LANES] = natural.astype(jnp.bfloat16)


def by_bins(records, first_station, second_region, second_station):
    regions, slabs = lax.axis_size("region"), lax.axis_size("slab")
    devices = regions * slabs
    stations, samples = records.shape
    parts = slabs // SEG
    rows = stations // parts
    count = rows // 2
    pair_count = first_station.shape[0]
    vmem = pl.BlockSpec(memory_space=pltpu.VMEM)
    limit = pltpu.CompilerParams(vmem_limit_bytes=12 << 20)
    divided = pl.pallas_call(
        divide_kernel,
        out_shape=[jax.ShapeDtypeStruct((rows, samples), records.dtype)] * parts,
        in_specs=[vmem],
        out_specs=[vmem] * parts,
        compiler_params=limit,
        name="divide",
    )(records)
    arrived = list(divided)
    for k in range(parts - 1, 0, -1):
        arrived[k] = lax.ppermute(divided[k], "slab", [(i, i ^ k) for i in range(slabs)])
    named = first_station + EXACT * second_station + EXACT * EXACT * second_region.reshape(-1)
    prepared = pl.pallas_call(
        prepare_kernel,
        out_shape=[
            jax.ShapeDtypeStruct((INDEX_ROWS, pair_count), jnp.bfloat16),
            jax.ShapeDtypeStruct((TAPER_ROWS, samples), jnp.float32),
            jax.ShapeDtypeStruct((CLASSES * samples, 2 * WIDTH), jnp.bfloat16),
        ],
        in_specs=[vmem] * 2,
        out_specs=[vmem] * 3,
        compiler_params=limit,
        cost_estimate=pl.CostEstimate(flops=NFFT * BINS, bytes_accessed=NFFT * BINS, transcendentals=0),
        name="prepare",
    )(named.reshape(1, -1), jnp.asarray(constant_rows()))
    sent = pl.pallas_call(
        spectra_kernel,
        out_shape=jax.ShapeDtypeStruct((devices * (count + INDEX_ROWS), LANES), jnp.bfloat16),
        in_specs=[vmem] * (parts + 3),
        out_specs=vmem,
        compiler_params=limit,
        name="spectra",
    )(*arrived, *prepared)
    blocks = sent.reshape(devices, (count + INDEX_ROWS) // INDEX_ROWS, INDEX_ROWS, LANES)
    table = lax.all_to_all(blocks, AXES, split_axis=0, concat_axis=0, tiled=True, axis_index_groups=[SPECTRA_RANKS]).reshape(sent.shape)
    partial = pl.pallas_call(
        functools.partial(cross_kernel, regions, slabs),
        out_shape=jax.ShapeDtypeStruct((devices, LANES // 2, pair_count), jnp.bfloat16),
        in_specs=[vmem],
        out_specs=vmem,
        scratch_shapes=[pltpu.VMEM((regions * LANES, stations), jnp.bfloat16)],
        compiler_params=limit,
        name="cross",
    )(table)
    pieces = lax.all_to_all(partial, AXES, split_axis=0, concat_axis=0, tiled=True, axis_index_groups=[RESULT_RANKS])
    return pl.pallas_call(
        place_kernel,
        out_shape=jax.ShapeDtypeStruct((pair_count, 2 * BINS), jnp.bfloat16),
        in_specs=[vmem],
        out_specs=vmem,
        compiler_params=limit,
        name="place",
    )(pieces)


def dft_table():
    sample = jnp.arange(NFFT, dtype=jnp.int32)[:, None]
    frequency = jnp.arange(BINS, dtype=jnp.int32)[None, :]
    phase = (sample * frequency % NFFT).astype(jnp.float32) * (2.0 * math.pi / NFFT)
    return jnp.concatenate([jnp.cos(phase), -jnp.sin(phase)], axis=1).astype(jnp.bfloat16)


def whitened(traces):
    count = traces.shape[0]
    signal = traces.astype(jnp.float32).reshape(count * SEG, NFFT)
    signal = signal - jnp.mean(signal, axis=1, keepdims=True)
    position = jnp.arange(NFFT, dtype=jnp.int32).astype(jnp.float32)
    taper = 0.5 - 0.5 * jnp.cos(position * (2.0 * math.pi / NFFT))
    tapered = (signal * taper[None, :]).astype(jnp.bfloat16)
    spectrum = jnp.dot(tapered, dft_table(), preferred_element_type=jnp.float32)
    real_part = spectrum[:, :BINS]
    imag_part = spectrum[:, BINS:]
    amplitude = jnp.sqrt(real_part * real_part + imag_part * imag_part + 1e-06)
    padded = jnp.pad(amplitude, ((0, 0), (HALF, HALF)))
    smooth = jnp.zeros_like(amplitude)
    for offset in range(2 * HALF + 1):
        smooth = smooth + padded[:, offset : offset + BINS]
    smooth = smooth / (2 * HALF + 1)
    level = jnp.mean(amplitude, axis=1, keepdims=True)
    divisor = smooth + level + 1e-06
    white = spectrum / jnp.concatenate([divisor, divisor], axis=1)
    return white.astype(jnp.bfloat16).reshape(count, SEG * NFFT)


def cross(first_rows, second_rows):
    left = first_rows.astype(jnp.float32).reshape(first_rows.shape[:-1] + (SEG, 2, BINS))
    right = second_rows.astype(jnp.float32).reshape(second_rows.shape[:-1] + (SEG, 2, BINS))
    real_sum = jnp.mean(left[..., 0, :] * right[..., 0, :] + left[..., 1, :] * right[..., 1, :], axis=-2)
    imag_sum = jnp.mean(left[..., 0, :] * right[..., 1, :] - left[..., 1, :] * right[..., 0, :], axis=-2)
    return jnp.concatenate([real_sum, imag_sum], axis=-1).astype(jnp.bfloat16)


def by_rows(records, first_station, second_region, second_station):
    regions = lax.axis_size("region")
    pair_count = first_station.shape[0]
    capacity = max(2, pair_count // regions + pair_count // 16)
    arrived = lax.all_to_all(records, "slab", split_axis=0, concat_axis=1, tiled=True)
    spectra = whitened(arrived)
    width = spectra.shape[1]
    target = second_region[:, 0]
    onehot = (target[:, None] == jnp.arange(regions, dtype=jnp.int32)[None, :]).astype(jnp.int32)
    ranking = jnp.sum((jnp.cumsum(onehot, axis=0) - onehot) * onehot, axis=1)
    slot_index = target * capacity + ranking
    requests = jnp.zeros((regions * capacity,), jnp.int32).at[slot_index].set(second_station).reshape(regions, capacity)
    incoming = lax.all_to_all(requests, "region", split_axis=0, concat_axis=0, tiled=True)
    wanted = jnp.concatenate([first_station, incoming.reshape(-1)])
    piece = lax.all_gather(spectra, "slab", axis=0, tiled=True)
    picked = jnp.take(piece, wanted, axis=0)
    first_rows = picked[:pair_count]
    served = picked[pair_count:]
    returned = lax.all_to_all(
        served.reshape(regions, capacity, width), "region", split_axis=0, concat_axis=0, tiled=True
    )
    second_rows = jnp.take(returned.reshape(regions * capacity, width), slot_index, axis=0)
    return cross(first_rows, second_rows)


def local(records, first_station, second_region, second_station):
    slabs = lax.axis_size("slab")
    devices = lax.axis_size("region") * slabs
    fits = (
        devices * LANES == 4 * BINS
        and devices == len(SPECTRA_RANKS)
        and records.shape == (EXACT, NFFT * SEG // slabs)
        and slabs == 4 * SEG
        and first_station.shape[0] == LANES
    )
    plan = by_bins if fits else by_rows
    return plan(records, first_station, second_region, second_station)


def solution(mesh):
    placed = (
        P(AXES[0], AXES[1]),
        P(AXES),
        P(AXES, None),
        P(AXES),
    )
    return jax.shard_map(local, mesh=mesh, in_specs=placed, out_specs=P(AXES, None), check_vma=False)
```

```python
import functools
import math

import jax
import jax.numpy as jnp
import numpy as np
from jax import lax
from jax.experimental import pallas as pl
from jax.experimental.pallas import tpu as pltpu
from jax.sharding import PartitionSpec as P

NFFT = 2048
BINS = 1024
SEG = 2
HALF = 4
LANES = 128
INDEX_ROWS = 4
CLASSES = 4
WIDTH = BINS // CLASSES
COARSE, FINE = 16, 32
TAPER_ROWS = 8
EXACT = 256
AXES = ("region", "slab")
SPECTRA_RANKS = [
    16, 8, 24, 0, 15, 23, 7, 31, 26, 10, 18, 2, 19, 11, 27, 3,
    20, 13, 28, 4, 21, 12, 29, 5, 22, 14, 30, 6, 17, 9, 25, 1,
]
RESULT_RANKS = [
    16, 0, 8, 24, 17, 13, 21, 29, 15, 23, 7, 31, 3, 11, 19, 27,
    1, 9, 5, 20, 2, 18, 10, 26, 6, 14, 22, 30, 4, 12, 25, 28,
]


def constant_rows():
    rows = []
    for pair in range(CLASSES // 2):
        frequency = np.concatenate([CLASSES * np.arange(WIDTH, dtype=np.int64) + 2 * pair + side for side in (0, 1)])
        for sample in (FINE * np.arange(COARSE, dtype=np.int64), np.arange(FINE, dtype=np.int64)):
            phase = (sample[:, None] * frequency[None, :] % NFFT) * (2.0 * math.pi / NFFT)
            rows += [np.cos(phase), np.sin(phase)]
    angle = np.arange(NFFT, dtype=np.float32) * np.float32(2.0 * math.pi / NFFT)
    cosine = np.cos(angle.astype(np.float64)).astype(np.float32)
    taper = (np.float32(0.5) - np.float32(0.5) * cosine).reshape(CLASSES, -1)
    rows.append(np.pad(taper, ((0, TAPER_ROWS - CLASSES), (0, 0))))
    return np.concatenate(rows, axis=0).astype(np.float32)


def prepare_kernel(named_ref, rows_ref, index_ref, taper_ref, table_ref):
    row = lax.broadcasted_iota(jnp.int32, index_ref.shape, 0)
    named = lax.rem(jnp.right_shift(named_ref[...], 8 * row), EXACT)
    index_ref[...] = named.astype(jnp.float32).astype(jnp.bfloat16)
    held = 2 * (COARSE + FINE)
    taper_ref[...] = rows_ref[held * CLASSES // 2 :, :]
    for pair in range(CLASSES // 2):
        at = pair * held
        fine_cos = rows_ref[at + 2 * COARSE : at + 2 * COARSE + FINE, :]
        fine_sin = rows_ref[at + 2 * COARSE + FINE : at + held, :]

        def block(i, _):
            coarse_cos = rows_ref[pl.ds(at + i, 1), :]
            coarse_sin = rows_ref[pl.ds(at + COARSE + i, 1), :]
            cosine = (coarse_cos * fine_cos - coarse_sin * fine_sin).astype(jnp.bfloat16)
            sine = (-coarse_sin * fine_cos - coarse_cos * fine_sin).astype(jnp.bfloat16)
            for side in (0, 1):
                first = (2 * pair + side) * FINE * COARSE + i * FINE
                place = pl.ds(pl.multiple_of(first, FINE), FINE)
                table_ref[place, :WIDTH] = cosine[:, side * WIDTH : (side + 1) * WIDTH]
                table_ref[place, WIDTH:] = sine[:, side * WIDTH : (side + 1) * WIDTH]
            return 0

        lax.fori_loop(0, COARSE, block, 0, unroll=4)


def divide_kernel(records_ref, *targets):
    parts = len(targets)
    rows = targets[0].shape[0]
    own = lax.rem(lax.axis_index("slab"), parts)
    for k, target in enumerate(targets):
        first = pl.multiple_of(jnp.bitwise_xor(own, k) * rows, rows)
        target[...] = records_ref[pl.ds(first, rows), :]


def shifted(values, step):
    width = values.shape[1]
    lane = lax.broadcasted_iota(jnp.int32, values.shape, 1)
    moved = pltpu.roll(values, (-step) % width, 1)
    return jnp.where((lane + step >= 0) & (lane + step < width), moved, 0.0)


def two_terms(values):
    coarse = values.astype(jnp.bfloat16)
    fine = (values - coarse.astype(jnp.float32)).astype(jnp.bfloat16)
    return jnp.concatenate([coarse, fine], axis=0)


def spectra_kernel(*refs):
    parts = len(refs) - 4
    index_ref, taper_ref, table_ref, out_ref = refs[parts:]
    rows, samples = refs[0].shape
    count = rows // 2
    own = lax.rem(lax.axis_index("slab"), parts)
    blocks = [ref[...] for ref in refs[:parts]]
    for bit in range(parts.bit_length() - 1):
        swapped = jnp.bitwise_and(jnp.right_shift(own, bit), 1) == 1
        blocks = [jnp.where(swapped, blocks[k ^ (1 << bit)], blocks[k]) for k in range(parts)]
    blocks = [block.astype(jnp.float32) for block in blocks]
    mean = jnp.sum((blocks[0] + blocks[1]) + (blocks[2] + blocks[3]), axis=1, keepdims=True) * (1.0 / NFFT)
    blocks = [((block - mean) * taper_ref[j : j + 1, :]).astype(jnp.bfloat16) for j, block in enumerate(blocks)]
    blocks = [block.astype(jnp.float32) for block in blocks]

    def transformed(values, r):
        table = table_ref[r * samples : (r + 1) * samples, :]
        both = jnp.dot(two_terms(values), table, preferred_element_type=jnp.float32)
        both = both[: values.shape[0]] + both[values.shape[0] :]
        return both[:, :WIDTH], both[:, WIDTH:]

    added, taken = ([blocks[j] + sign * blocks[j + 2] for j in (0, 1)] for sign in (1.0, -1.0))
    spectrum = [None] * CLASSES
    spectrum[0] = transformed(added[0] + added[1], 0)
    spectrum[2] = transformed(added[0] - added[1], 2)
    for r, sign in ((1, 1.0), (3, -1.0)):
        with_cos, with_sin = transformed(jnp.concatenate(taken, axis=0), r)
        spectrum[r] = (with_cos[:rows] + sign * with_sin[rows:], with_sin[:rows] - sign * with_cos[rows:])
    size = [jnp.sqrt(re * re + im * im + 1e-06) for re, im in spectrum]
    every = (size[0] + size[1]) + (size[2] + size[3])
    level = jnp.sum(every, axis=1, keepdims=True) * (1.0 / BINS) + 1e-06
    before, after = ([shifted(part, step) for part in size] for step in (-1, 1))
    group = LANES // 4
    lane_group = lax.broadcasted_iota(jnp.int32, (count, LANES), 1) // group
    for r in range(CLASSES):
        smooth = every
        for part in before[r:] + after[: r + 1]:
            smooth = smooth + part
        scale = 1.0 / (smooth * (1.0 / (2 * HALF + 1)) + level)
        white = [(part * scale).astype(jnp.bfloat16) for part in spectrum[r]]
        for s in range(WIDTH // LANES):
            sources = [
                part[side * count : (side + 1) * count, s * LANES : (s + 1) * LANES] for side in (0, 1) for part in white
            ]
            for q in range(4):
                block = None
                for place, source in enumerate(sources):
                    turn = (place - q) * group % LANES
                    moved = pltpu.roll(source, turn, 1) if turn else source
                    block = moved if block is None else jnp.where(lane_group == place, moved, block)
                at = (r * WIDTH // group + 4 * s + q) * (count + INDEX_ROWS)
                out_ref[at : at + count, :] = block
                out_ref[at + count : at + count + INDEX_ROWS, :] = index_ref[...]


def cross_kernel(regions, slabs, table_ref, out_ref, flipped_ref):
    devices = regions * slabs
    rows = table_ref.shape[0] // devices
    count = rows - INDEX_ROWS
    parts = slabs // SEG
    wide = parts * count
    stations = 2 * wide
    bins = LANES // 4
    per_step = 2
    for region in range(regions):
        for segment in range(SEG):
            sources = [SPECTRA_RANKS.index(region * slabs + segment * parts + part) * rows for part in range(parts)]
            block = jnp.concatenate([table_ref[at : at + count, :] for at in sources], axis=0).T
            at = region * LANES + segment * 2 * bins
            for half in (0, 1):
                flipped_ref[at : at + 2 * bins, half * wide : (half + 1) * wide] = block[half * 2 * bins : (half + 1) * 2 * bins]
    column = lax.broadcasted_iota(jnp.int32, (stations, per_step * LANES), 0)
    half, part = column // wide, column % wide // count
    station = (part * 2 + half) * count + column % count
    station = station.astype(jnp.float32).astype(jnp.bfloat16)
    one, zero = jnp.ones((), jnp.bfloat16), jnp.zeros((), jnp.bfloat16)
    for i in range(devices // per_step):
        home, first_slab = i % regions, i // regions * per_step
        owners = [home * slabs + first_slab + k for k in range(per_step)]
        places = [SPECTRA_RANKS.index(owner) * rows for owner in owners]
        named = [table_ref[at + count : at + rows, :] for at in places]
        named = jnp.concatenate(named, axis=1)
        first, second, target = named[0:1], named[1:2], named[2:3].astype(jnp.float32)
        own = flipped_ref[home * LANES : (home + 1) * LANES, :]
        a = jnp.dot(own, jnp.where(station == first, one, zero), preferred_element_type=jnp.float32)
        pick_second = jnp.where(station == second, one, zero)
        b = None
        for region in range(regions):
            rows_of = flipped_ref[region * LANES : (region + 1) * LANES, :]
            candidate = jnp.dot(rows_of, pick_second, preferred_element_type=jnp.float32)
            b = candidate if b is None else jnp.where(target == region, candidate, b)
        real_sum, imag_sum = 0.0, 0.0
        for segment in range(SEG):
            at = 2 * segment * bins
            ar, ai = a[at : at + bins], a[at + bins : at + 2 * bins]
            br, bi = b[at : at + bins], b[at + bins : at + 2 * bins]
            real_sum = real_sum + (ar * br + ai * bi)
            imag_sum = imag_sum + (ar * bi - ai * br)
        real_sum = (real_sum * (1.0 / SEG)).astype(jnp.bfloat16)
        imag_sum = (imag_sum * (1.0 / SEG)).astype(jnp.bfloat16)
        for k, owner in enumerate(owners):
            at = RESULT_RANKS.index(owner)
            out_ref[at, :bins, :] = real_sum[:, k * LANES : (k + 1) * LANES]
            out_ref[at, bins:, :] = imag_sum[:, k * LANES : (k + 1) * LANES]


def place_kernel(in_ref, out_ref):
    devices, rows, _ = in_ref.shape
    bins = rows // 2
    row = lax.broadcasted_iota(jnp.int32, (LANES, LANES), 0)
    lane = lax.broadcasted_iota(jnp.int32, (LANES, LANES), 1)
    order = (lane == CLASSES * (row % bins) + row // bins).astype(jnp.float32).astype(jnp.bfloat16)
    for kind in (0, 1):
        for j in range(devices // CLASSES):
            sources = range(j, devices, devices // CLASSES)
            places = [RESULT_RANKS.index(SPECTRA_RANKS[u]) for u in sources]
            block = jnp.concatenate([in_ref[at, kind * bins : (kind + 1) * bins, :] for at in places], axis=0).T
            natural = jnp.dot(block, order, preferred_element_type=jnp.float32)
            place = kind * BINS + j * LANES
            out_ref[:, place : place + LANES] = natural.astype(jnp.bfloat16)


def by_bins(records, first_station, second_region, second_station):
    regions, slabs = lax.axis_size("region"), lax.axis_size("slab")
    devices = regions * slabs
    stations, samples = records.shape
    parts = slabs // SEG
    rows = stations // parts
    count = rows // 2
    pair_count = first_station.shape[0]
    vmem = pl.BlockSpec(memory_space=pltpu.VMEM)
    limit = pltpu.CompilerParams(vmem_limit_bytes=12 << 20)
    divided = pl.pallas_call(
        divide_kernel,
        out_shape=[jax.ShapeDtypeStruct((rows, samples), records.dtype)] * parts,
        in_specs=[vmem],
        out_specs=[vmem] * parts,
        compiler_params=limit,
        name="divide",
    )(records)
    arrived = list(divided)
    for k in range(parts - 1, 0, -1):
        arrived[k] = lax.ppermute(divided[k], "slab", [(i, i ^ k) for i in range(slabs)])
    named = first_station + EXACT * second_station + EXACT * EXACT * second_region.reshape(-1)
    prepared = pl.pallas_call(
        prepare_kernel,
        out_shape=[
            jax.ShapeDtypeStruct((INDEX_ROWS, pair_count), jnp.bfloat16),
            jax.ShapeDtypeStruct((TAPER_ROWS, samples), jnp.float32),
            jax.ShapeDtypeStruct((CLASSES * samples, 2 * WIDTH), jnp.bfloat16),
        ],
        in_specs=[vmem] * 2,
        out_specs=[vmem] * 3,
        compiler_params=limit,
        cost_estimate=pl.CostEstimate(flops=NFFT * BINS, bytes_accessed=NFFT * BINS, transcendentals=0),
        name="prepare",
    )(named.reshape(1, -1), jnp.asarray(constant_rows()))
    sent = pl.pallas_call(
        spectra_kernel,
        out_shape=jax.ShapeDtypeStruct((devices * (count + INDEX_ROWS), LANES), jnp.bfloat16),
        in_specs=[vmem] * (parts + 3),
        out_specs=vmem,
        compiler_params=limit,
        name="spectra",
    )(*arrived, *prepared)
    blocks = sent.reshape(devices, (count + INDEX_ROWS) // INDEX_ROWS, INDEX_ROWS, LANES)
    table = lax.all_to_all(blocks, AXES, split_axis=0, concat_axis=0, tiled=True, axis_index_groups=[SPECTRA_RANKS]).reshape(sent.shape)
    partial = pl.pallas_call(
        functools.partial(cross_kernel, regions, slabs),
        out_shape=jax.ShapeDtypeStruct((devices, LANES // 2, pair_count), jnp.bfloat16),
        in_specs=[vmem],
        out_specs=vmem,
        scratch_shapes=[pltpu.VMEM((regions * LANES, stations), jnp.bfloat16)],
        compiler_params=limit,
        name="cross",
    )(table)
    pieces = lax.all_to_all(partial, AXES, split_axis=0, concat_axis=0, tiled=True, axis_index_groups=[RESULT_RANKS])
    return pl.pallas_call(
        place_kernel,
        out_shape=jax.ShapeDtypeStruct((pair_count, 2 * BINS), jnp.bfloat16),
        in_specs=[vmem],
        out_specs=vmem,
        compiler_params=limit,
        name="place",
    )(pieces)


def dft_table():
    sample = jnp.arange(NFFT, dtype=jnp.int32)[:, None]
    frequency = jnp.arange(BINS, dtype=jnp.int32)[None, :]
    phase = (sample * frequency % NFFT).astype(jnp.float32) * (2.0 * math.pi / NFFT)
    return jnp.concatenate([jnp.cos(phase), -jnp.sin(phase)], axis=1).astype(jnp.bfloat16)


def whitened(traces):
    count = traces.shape[0]
    signal = traces.astype(jnp.float32).reshape(count * SEG, NFFT)
    signal = signal - jnp.mean(signal, axis=1, keepdims=True)
    position = jnp.arange(NFFT, dtype=jnp.int32).astype(jnp.float32)
    taper = 0.5 - 0.5 * jnp.cos(position * (2.0 * math.pi / NFFT))
    tapered = (signal * taper[None, :]).astype(jnp.bfloat16)
    spectrum = jnp.dot(tapered, dft_table(), preferred_element_type=jnp.float32)
    real_part = spectrum[:, :BINS]
    imag_part = spectrum[:, BINS:]
    amplitude = jnp.sqrt(real_part * real_part + imag_part * imag_part + 1e-06)
    padded = jnp.pad(amplitude, ((0, 0), (HALF, HALF)))
    smooth = jnp.zeros_like(amplitude)
    for offset in range(2 * HALF + 1):
        smooth = smooth + padded[:, offset : offset + BINS]
    smooth = smooth / (2 * HALF + 1)
    level = jnp.mean(amplitude, axis=1, keepdims=True)
    divisor = smooth + level + 1e-06
    white = spectrum / jnp.concatenate([divisor, divisor], axis=1)
    return white.astype(jnp.bfloat16).reshape(count, SEG * NFFT)


def cross(first_rows, second_rows):
    left = first_rows.astype(jnp.float32).reshape(first_rows.shape[:-1] + (SEG, 2, BINS))
    right = second_rows.astype(jnp.float32).reshape(second_rows.shape[:-1] + (SEG, 2, BINS))
    real_sum = jnp.mean(left[..., 0, :] * right[..., 0, :] + left[..., 1, :] * right[..., 1, :], axis=-2)
    imag_sum = jnp.mean(left[..., 0, :] * right[..., 1, :] - left[..., 1, :] * right[..., 0, :], axis=-2)
    return jnp.concatenate([real_sum, imag_sum], axis=-1).astype(jnp.bfloat16)


def by_rows(records, first_station, second_region, second_station):
    regions = lax.axis_size("region")
    pair_count = first_station.shape[0]
    capacity = max(2, pair_count // regions + pair_count // 16)
    arrived = lax.all_to_all(records, "slab", split_axis=0, concat_axis=1, tiled=True)
    spectra = whitened(arrived)
    width = spectra.shape[1]
    target = second_region[:, 0]
    onehot = (target[:, None] == jnp.arange(regions, dtype=jnp.int32)[None, :]).astype(jnp.int32)
    ranking = jnp.sum((jnp.cumsum(onehot, axis=0) - onehot) * onehot, axis=1)
    slot_index = target * capacity + ranking
    requests = jnp.zeros((regions * capacity,), jnp.int32).at[slot_index].set(second_station).reshape(regions, capacity)
    incoming = lax.all_to_all(requests, "region", split_axis=0, concat_axis=0, tiled=True)
    wanted = jnp.concatenate([first_station, incoming.reshape(-1)])
    piece = lax.all_gather(spectra, "slab", axis=0, tiled=True)
    picked = jnp.take(piece, wanted, axis=0)
    first_rows = picked[:pair_count]
    served = picked[pair_count:]
    returned = lax.all_to_all(
        served.reshape(regions, capacity, width), "region", split_axis=0, concat_axis=0, tiled=True
    )
    second_rows = jnp.take(returned.reshape(regions * capacity, width), slot_index, axis=0)
    return cross(first_rows, second_rows)


def local(records, first_station, second_region, second_station):
    slabs = lax.axis_size("slab")
    devices = lax.axis_size("region") * slabs
    fits = (
        devices * LANES == 4 * BINS
        and devices == len(SPECTRA_RANKS)
        and records.shape == (EXACT, NFFT * SEG // slabs)
        and slabs == 4 * SEG
        and first_station.shape[0] == LANES
    )
    plan = by_bins if fits else by_rows
    return plan(records, first_station, second_region, second_station)


def solution(mesh):
    placed = (
        P(AXES[0], AXES[1]),
        P(AXES),
        P(AXES, None),
        P(AXES),
    )
    return jax.shard_map(local, mesh=mesh, in_specs=placed, out_specs=P(AXES, None), check_vma=False)
```
